128 devices in a mesh: enc: 16 (over x, y), dec: 4 (over z), ret: 2 (over core).
Axes of the slice: x: 4, y: 4, z: 4, core: 2. Of those that a mesh axis runs over, the one named last changes fastest.
Arguments:
- enc_states: bfloat16 [32, 2, 256, 4096], P('enc', 'ret'), may hold values from -22 to 22
- kv_weight: bfloat16 [4096, 64, 128], P(None, 'dec'), may hold values from -1 to 1
- queries: bfloat16 [8, 128, 64, 64], P('ret', None, ('dec', 'enc')), may hold values from -47 to 47
- out_grad: bfloat16 [8, 128, 64, 64], P('ret', None, ('dec', 'enc')), may hold values from -6 to 6
- passage_order: int32 [2, 32], P('ret'), may hold values from 0 to 31, each once within a row
- passage_blocks: int32 [2, 32], P('ret'), may hold values from 1 to 2
- ret_tokens: bfloat16 [32, 2, 256, 768], P('enc', 'ret'), may hold values from -6 to 6
- ret_weight: bfloat16 [768, 768], replicated, may hold values from -0.21875 to 0.21875
- question_emb: float32 [8, 768], P('ret'), may hold values from -7 to 7
Outputs:
- kv_grad: bfloat16 [32, 2, 256, 64, 128], P('enc', 'ret', None, 'dec')
- kv_weight_grad: bfloat16 [4096, 64, 128], P(('enc', 'ret'), 'dec')
- ret_weight_grad: bfloat16 [768, 768], replicated
The draws below stay inside these ranges and needn't reach their ends.
Inputs may be any that keep to these rules, and one draw needn't show every extreme that they name: `passage_order`: each row lists every passage of its group once; slots i * 8 to (i + 1) * 8 - 1 belong to question i of the group.
All inputs are finite; a program needn't handle non-finite values.
Results may differ from the reference program's by a relative error of at most 0.025.
Values may be sent and summed in bfloat16 or wider, within the bound.
No kernel may reach another device: no remote copies, remote signals or barrier semaphores. Data moves between devices by JAX's collectives and lax.ppermute only.
A program may use at most 128 MiB of HBM per device.

```python
import math
import jax
import jax.numpy as jnp
from jax import lax

D = 4096
HEADS = 64
HD = 64
RD = 768
BLK = 128
MAXB = 2
PASS = 8
P_DEV = 2
LQ = 128
SLOT = 256
GP = 32
QG = 4
QUESTIONS = 8
N_ENC = 16
N_RET = 2


def shared_directions(key):
    along_model = jnp.clip(jax.random.normal(jax.random.fold_in(key, 9101), (D,), jnp.float32), -3.0, 3.0)
    along_head = jnp.clip(jax.random.normal(jax.random.fold_in(key, 9102), (HEADS, HD), jnp.float32), -3.0, 3.0)
    return (along_model, along_head)


def draw_enc_states(key, part):
    along_model, along_head = shared_directions(key)
    noise_key = jax.random.fold_in(key, 9201)
    noise = jnp.clip(jax.random.normal(noise_key, (GP, N_RET, SLOT, D), jnp.float32), -4.5, 4.5)
    enc_blocks = GP // P_DEV
    pairing = jax.random.permutation(jax.random.fold_in(key, 9202), enc_blocks)
    passage_block = jnp.arange(GP, dtype=jnp.int32) // P_DEV
    width_block = jnp.arange(D, dtype=jnp.int32) // (D // enc_blocks)
    matched = pairing[passage_block][:, None] == width_block[None, :]
    boost = jnp.where(matched, 3.0, 1.0).astype(jnp.float32)[:, None, None, :]
    passage_offset = jax.random.uniform(jax.random.fold_in(key, 9204), (GP, N_RET, 1, 1), jnp.float32, -1.5, 1.5)
    return (noise * boost + (1.0 + passage_offset) * along_model[None, None, None, :]).astype(jnp.bfloat16)


def draw_kv_weight(key, part):
    along_model, along_head = shared_directions(key)
    noise_key = jax.random.fold_in(key, 9251)
    noise = jnp.clip(jax.random.normal(noise_key, (D, HEADS, 2 * HD), jnp.float32), -5.0, 5.0)
    noise = noise / jnp.sqrt(jnp.float32(D))
    key_common = 2.0 * along_model[:, None, None] * along_head[None, :, :] / D
    common = jnp.concatenate([key_common, jnp.zeros((D, HEADS, HD), jnp.float32)], axis=-1)
    return (noise + common).astype(jnp.bfloat16)


def draw_queries(key, part):
    along_model, along_head = shared_directions(key)
    noise_key = jax.random.fold_in(key, 9301)
    noise = jnp.clip(jax.random.normal(noise_key, (QUESTIONS, LQ, HEADS, HD), jnp.float32), -4.5, 4.5)
    head_pick = jax.random.randint(jax.random.fold_in(key, 9302), (QUESTIONS,), 0, HEADS)
    ranking = jax.random.permutation(jax.random.fold_in(key, 9303), QUESTIONS)
    levels = jnp.array([14.0, 10.0, 7.0], jnp.float32)
    strength = levels[ranking % 3]
    picked = (jnp.arange(HEADS, dtype=jnp.int32)[None, :] == head_pick[:, None]).astype(jnp.float32) * strength[:, None]
    lifted = picked[:, None, :, None] * along_head[None, None, :, :]
    return (noise + lifted).astype(jnp.bfloat16)


def draw_question_emb(key, part):
    noise_key = jax.random.fold_in(key, 9401)
    noise = jnp.clip(jax.random.normal(noise_key, (QUESTIONS, RD), jnp.float32), -4.5, 4.5)
    ranking = jax.random.permutation(jax.random.fold_in(key, 9402), QUESTIONS)
    lifted_count = max(1, QUESTIONS * 3 // 8)
    levels = jnp.array([1.8, 1.1, 0.6], jnp.float32)
    lift = jnp.where(ranking < lifted_count, levels[ranking % 3], 0.0)
    return (noise + lift[:, None]).astype(jnp.float32)


def plant(values, own_key, smallest, high):
    dims = values.shape
    spot = [jax.random.randint(jax.random.fold_in(own_key, axis), (), 0, dims[axis]) for axis in range(len(dims))]
    values = values.at[tuple(spot)].set(smallest)
    longest = dims.index(max(dims))
    spot[longest] = (spot[longest] + 1) % dims[longest]
    return values.at[tuple(spot)].set(high)


def shard_levels(rng, shape, shards, low, top_value):
    loudness, own = 1.0, jax.random.fold_in(rng, 6)
    for position, parts in shards:
        steps = jnp.exp(jax.random.uniform(jax.random.fold_in(own, position), (parts,), jnp.float32, low / len(shards), top_value / len(shards)))
        loudness = loudness * jnp.repeat(steps, shape[position] // parts).reshape([-1 if axis == position else 1 for axis in range(len(shape))])
    return loudness


def bell_draw(rng, dims, width, bound, split=(), kind=jnp.bfloat16):
    entries = width * jax.random.normal(rng, dims, jnp.float32)
    if split:
        entries = entries * shard_levels(rng, dims, split, -0.22, 0.18)
    return jnp.clip(entries, -bound, bound).astype(kind)


def setup_inputs(seed: int = 0) -> dict:
    key_of = jax.random.split(jax.random.key(seed), 10)
    return {
        "enc_states": draw_enc_states(jax.random.fold_in(key_of[9], 71), 0),
        "kv_weight": draw_kv_weight(jax.random.fold_in(key_of[9], 71), 0),
        "queries": draw_queries(jax.random.fold_in(key_of[9], 71), 0),
        "out_grad": bell_draw(key_of[3], (QUESTIONS, LQ, HEADS, HD), 1.0, 6.0, ((0, 2), (2, 64))),
        "passage_order": jax.vmap(lambda own: jax.random.permutation(own, GP))(jax.random.split(key_of[4], N_RET)).reshape((N_RET, GP)).astype(jnp.int32),
        "passage_blocks": plant(jax.random.randint(key_of[5], (N_RET, GP), 1, MAXB + 1), jax.random.fold_in(key_of[5], 1), 1, MAXB).astype(jnp.int32),
        "ret_tokens": bell_draw(key_of[6], (GP, N_RET, SLOT, RD), 1.0, 6.0, ((0, 16), (1, 2))),
        "ret_weight": bell_draw(key_of[7], (RD, RD), RD ** -0.5, 0.21875),
        "question_emb": draw_question_emb(jax.random.fold_in(key_of[9], 71), 0),
    }


def gelu_grad(pre_act, upstream):
    return jax.vjp(jax.nn.gelu, pre_act)[1](upstream)[0]

def reference(enc_states, kv_weight, queries, out_grad, passage_order, passage_blocks, ret_tokens, ret_weight, question_emb):
    key_value = jnp.dot(enc_states.reshape(-1, D), kv_weight.reshape(D, HEADS * 2 * HD), preferred_element_type=jnp.float32)
    key_value = key_value.reshape(GP, N_RET, SLOT, HEADS, 2 * HD)
    positions = jnp.arange(SLOT, dtype=jnp.int32)
    live = positions[None, None, :] < BLK * jnp.transpose(passage_blocks)[:, :, None]
    order_rows = passage_order.reshape(QUESTIONS, PASS)
    group_rows = jnp.broadcast_to((jnp.arange(QUESTIONS, dtype=jnp.int32) // QG)[:, None], (QUESTIONS, PASS))
    scale = 1.0 / math.sqrt(HD)
    highest = lax.Precision.HIGHEST

    def per_question(number):
        group = number // QG
        chosen = order_rows[number]
        rows_kv = key_value[chosen, group].reshape(PASS * SLOT, HEADS, 2 * HD)
        live_keys = live[chosen, group].reshape(PASS * SLOT)
        keys = rows_kv[:, :, :HD]
        values = rows_kv[:, :, HD:]
        query_one = queries[number].astype(jnp.float32)
        grad_one = out_grad[number].astype(jnp.float32)
        scores = jnp.einsum('lhc,khc->hlk', query_one, keys, precision=highest) * scale
        masked = jnp.where(live_keys[None, None, :], scores, -1e+30)
        top = lax.optimization_barrier(jnp.max(masked, axis=-1, keepdims=True))
        expo = jnp.where(live_keys[None, None, :], jnp.exp(masked - top), 0.0)
        probs = expo / lax.optimization_barrier(jnp.sum(expo, axis=-1, keepdims=True))
        probs_low = probs.astype(jnp.bfloat16).astype(jnp.float32)
        attended = jnp.einsum('hlk,khc->lhc', probs_low, values, precision=highest)
        value_grad = jnp.einsum('hlk,lhc->khc', probs_low, grad_one)
        prob_grad = jnp.einsum('lhc,khc->hlk', grad_one, values, precision=highest)
        row_dot = jnp.einsum('lhc,lhc->hl', grad_one, attended)
        score_grad = (probs * (prob_grad - row_dot[:, :, None]) * scale).astype(jnp.bfloat16).astype(jnp.float32)
        key_grad = jnp.einsum('hlk,lhc->khc', score_grad, query_one)
        pair_grad = jnp.concatenate([key_grad, value_grad], axis=-1).astype(jnp.bfloat16)
        mass = lax.optimization_barrier(jnp.sum(probs, axis=(0, 1))).reshape(PASS, SLOT).sum(axis=-1) / (HEADS * LQ)
        return (pair_grad.reshape(PASS, SLOT, HEADS, 2 * HD), mass)
    grads_all, passage_mass = lax.map(per_question, jnp.arange(QUESTIONS, dtype=jnp.int32))
    kv_grad = jnp.zeros((GP, N_RET, SLOT, HEADS, 2 * HD), jnp.bfloat16).at[order_rows, group_rows].set(grads_all)
    states_blocks = enc_states.reshape(N_ENC, P_DEV, N_RET, SLOT, D)
    grad_blocks = kv_grad.reshape(N_ENC, P_DEV, N_RET, SLOT, HEADS * 2 * HD)

    def add_block(total, number):
        enc_part = number // N_RET
        ret_part = number % N_RET
        rows_left = states_blocks[enc_part][:, ret_part].reshape(P_DEV * SLOT, D)
        rows_right = grad_blocks[enc_part][:, ret_part].reshape(P_DEV * SLOT, HEADS * 2 * HD)
        partial_value = lax.dot_general(rows_left, rows_right, (((0,), (0,)), ((), ())), preferred_element_type=jnp.float32)
        return (total + lax.optimization_barrier(partial_value.astype(jnp.bfloat16)).astype(jnp.float32), None)
    weight_total, unused = lax.scan(add_block, jnp.zeros((D, HEADS * 2 * HD), jnp.float32), jnp.arange(N_ENC * N_RET, dtype=jnp.int32))
    kv_weight_grad = weight_total.astype(jnp.bfloat16).reshape(D, HEADS, 2 * HD)
    pre_act = jnp.dot(ret_tokens.reshape(-1, RD), ret_weight, preferred_element_type=jnp.float32).reshape(GP, N_RET, SLOT, RD)
    hidden = jax.nn.gelu(pre_act)
    lengths = (BLK * jnp.transpose(passage_blocks)).astype(jnp.float32)
    embed = lax.optimization_barrier(jnp.sum(jnp.where(live[..., None], hidden, 0.0), axis=2)) / lengths[..., None]
    chosen_embed = embed[order_rows, group_rows]
    ret_scores = lax.optimization_barrier(jnp.sum(question_emb[:, None, :] * chosen_embed, axis=-1))
    top_score = lax.optimization_barrier(jnp.max(ret_scores, axis=-1, keepdims=True))
    expo_score = jnp.exp(ret_scores - top_score)
    score_gap = expo_score / lax.optimization_barrier(jnp.sum(expo_score, axis=-1, keepdims=True)) - passage_mass
    gap_rows = score_gap[..., None] * question_emb[:, None, :]
    embed_grad = jnp.zeros((GP, N_RET, RD), jnp.float32).at[order_rows, group_rows].set(gap_rows)
    hidden_grad = jnp.where(live[..., None], (embed_grad / lengths[..., None])[:, :, None, :], 0.0)
    pre_grad = gelu_grad(pre_act, hidden_grad).astype(jnp.bfloat16)
    ret_weight_grad = lax.dot_general(ret_tokens.reshape(-1, RD), pre_grad.reshape(-1, RD), (((0,), (0,)), ((), ())), preferred_element_type=jnp.float32)
    return (kv_grad, kv_weight_grad, ret_weight_grad.astype(jnp.bfloat16))
```

```python
import functools

import jax
import jax.numpy as jnp
from jax import lax
from jax.experimental import pallas as pl
from jax.experimental.pallas import tpu as pltpu
from jax.sharding import PartitionSpec as P

BLK = 128
PASS = 8
N_ENC = 16
SIDE = 4
N_DEC = 4
LQ = 128
HD = 64
SLOT = 256
F32 = jnp.float32
BF16 = jnp.bfloat16
VMEM = 60 << 20


def gelu_grad(pre_act, upstream):
    return jax.vjp(jax.nn.gelu, pre_act)[1](upstream)[0]


def project_kernel(x_ref, w_ref, o_ref):
    @pl.when(pl.program_id(0) == 0)
    def _():
        o_ref[...] = jnp.zeros_like(o_ref)

    rows = x_ref[...]
    by_head = jnp.swapaxes(w_ref[...], 0, 1)
    for pair in range(by_head.shape[0] // 2):
        both = jnp.concatenate([by_head[2 * pair], by_head[2 * pair + 1]], axis=1)
        part = jnp.dot(rows, both, preferred_element_type=F32)
        o_ref[2 * pair] += part[:, :128]
        o_ref[2 * pair + 1] += part[:, 128:]


def project(tok_rows, kv_weight, depth=512):
    tokens, width = tok_rows.shape
    heads, pair_width = kv_weight.shape[1:]
    return pl.pallas_call(
        project_kernel,
        grid=(width // depth,),
        out_shape=jax.ShapeDtypeStruct((heads, tokens, pair_width), F32),
        in_specs=[
            pl.BlockSpec((tokens, depth), lambda i: (0, i)),
            pl.BlockSpec((depth, heads, pair_width), lambda i: (i, 0, 0)),
        ],
        out_specs=pl.BlockSpec((heads, tokens, pair_width), lambda i: (0, 0, 0)),
        compiler_params=pltpu.CompilerParams(vmem_limit_bytes=VMEM),
        cost_estimate=pl.CostEstimate(
            flops=2 * tokens * width * heads * pair_width,
            bytes_accessed=24 << 20,
            transcendentals=0,
        ),
        name="project",
    )(tok_rows, kv_weight)


def turn_kernel(rank_ref, x_ref, mine_ref, send_ref):
    rank = rank_ref[0]
    mine_ref[0] = x_ref[:, pl.ds(pl.multiple_of(rank * 128, 128), 128)].T
    send_ref[0] = x_ref[:, pl.ds(pl.multiple_of((1 - rank) * 128, 128), 128)].T


def turn(ret_rank, tok_rows):
    tokens, width = tok_rows.shape
    half = jax.ShapeDtypeStruct((N_ENC, 128, tokens), BF16)
    return pl.pallas_call(
        turn_kernel,
        grid_spec=pltpu.PrefetchScalarGridSpec(
            num_scalar_prefetch=1,
            grid=(N_ENC,),
            in_specs=[pl.BlockSpec((tokens, 256), lambda i, r: (0, i))],
            out_specs=[pl.BlockSpec((1, 128, tokens), lambda i, r: (i, 0, 0))] * 2,
        ),
        out_shape=[half, half],
        compiler_params=pltpu.CompilerParams(vmem_limit_bytes=VMEM),
        cost_estimate=pl.CostEstimate(flops=0, bytes_accessed=8 << 20, transcendentals=0),
        name="turn",
    )(ret_rank.reshape(1), tok_rows)


def local_scores(kv_ref, qd_ref, head, passage, question, blocks):
    pair = kv_ref[head, passage * SLOT : (passage + 1) * SLOT, :]
    high = pair.astype(BF16)
    low = (pair - high.astype(F32)).astype(BF16)
    rows = qd_ref[head, pl.ds(pl.multiple_of(question * LQ, LQ), LQ), :]
    lane = lax.broadcasted_iota(jnp.int32, rows.shape, 1)
    zero = jnp.zeros_like(rows)
    stacked = jnp.concatenate(
        [jnp.where(lane < HD, rows, zero), jnp.where(lane < HD, zero, rows)], axis=0
    )
    both = lax.dot_general(
        jnp.concatenate([high, low], axis=1),
        jnp.concatenate([stacked, stacked], axis=1),
        (((1,), (1,)), ((), ())),
        preferred_element_type=F32,
    )
    scores = both[:, :LQ]
    place = lax.broadcasted_iota(jnp.int32, scores.shape, 0)
    return jnp.where(place < BLK * blocks, scores, -1e30), both[:, LQ:], stacked


def stats_kernel(heads, question_ref, blocks_ref, kv_ref, qd_ref, score_ref, o_ref):
    step = pl.program_id(0)
    per_step = kv_ref.shape[0]

    @pl.when(step == 0)
    def _():
        o_ref[4 * heads :, :] = score_ref[...]

    for passage in range(2):
        tops, dots = [], []
        for head in range(per_step):
            scores, prob_grad, _ = local_scores(
                kv_ref, qd_ref, head, passage, question_ref[passage], blocks_ref[passage]
            )
            top = jnp.max(scores, axis=0, keepdims=True)
            expo = jnp.exp(scores - top)
            total = jnp.sum(expo, axis=0, keepdims=True)
            tops.append(top + jnp.log(total))
            dots.append(jnp.sum(expo * prob_grad, axis=0, keepdims=True) / total)
        place = passage * heads + step * per_step
        o_ref[pl.ds(pl.multiple_of(place, 8), per_step), :] = jnp.concatenate(tops, axis=0)
        o_ref[pl.ds(pl.multiple_of(2 * heads + place, 8), per_step), :] = jnp.concatenate(
            dots, axis=0
        )


def local_stats(own_question, own_blocks, key_value, gathered, score_rows):
    heads, tokens, pair_width = key_value.shape
    per_step = 8
    rows = 4 * heads + 8
    return pl.pallas_call(
        functools.partial(stats_kernel, heads),
        grid_spec=pltpu.PrefetchScalarGridSpec(
            num_scalar_prefetch=2,
            grid=(heads // per_step,),
            in_specs=[
                pl.BlockSpec((per_step, tokens, pair_width), lambda i, *_: (i, 0, 0)),
                pl.BlockSpec((per_step,) + gathered.shape[1:], lambda i, *_: (i, 0, 0)),
                pl.BlockSpec((8, 128), lambda i, *_: (0, 0)),
            ],
            out_specs=pl.BlockSpec((rows, 128), lambda i, *_: (0, 0)),
        ),
        out_shape=jax.ShapeDtypeStruct((rows, 128), F32),
        compiler_params=pltpu.CompilerParams(vmem_limit_bytes=VMEM),
        cost_estimate=pl.CostEstimate(
            flops=2 << 30, bytes_accessed=6 << 20, transcendentals=1 << 20
        ),
        name="local_stats",
    )(own_question, own_blocks, key_value, gathered, score_rows)


def back_kernel(
    heads,
    question_ref,
    blocks_ref,
    own_ref,
    order_ref,
    kv_ref,
    qd_ref,
    stats_ref,
    grad_ref,
    flat_ref,
    aux_ref,
    norm_ref,
):
    step = pl.program_id(0)
    per_step = kv_ref.shape[0]

    @pl.when(step == 0)
    def _():
        aux = []
        shares = []
        for passage in range(2):
            tops, dots, marks = [], [], []
            for slot in range(PASS):
                place = order_ref[question_ref[passage] * PASS + slot]
                owner = place // 2
                at = place - 2 * owner
                tops.append(
                    stats_ref[owner, pl.ds(pl.multiple_of(at * heads, heads), heads), :]
                )
                dots.append(
                    stats_ref[
                        owner,
                        pl.ds(pl.multiple_of((2 + at) * heads, heads), heads),
                        :,
                    ]
                )
                pair = stats_ref[owner, 4 * heads : 4 * heads + 8, :]
                marks.append(jnp.where(at == 0, pair[0:1], pair[1:2]))
            top = functools.reduce(jnp.maximum, tops)
            total = sum(jnp.exp(t - top) for t in tops)
            norm = top + jnp.log(total)
            norm_ref[passage] = norm
            norm_ref[2 + passage] = sum(jnp.exp(t - norm) * d for t, d in zip(tops, dots))
            own = stats_ref[own_ref[0], passage * heads : (passage + 1) * heads, :]
            mass = jnp.sum(jnp.exp(own - norm), axis=0, keepdims=True)
            aux.append(jnp.broadcast_to(jnp.sum(mass, axis=1, keepdims=True), (1, 128)))
            best = functools.reduce(jnp.maximum, marks)
            mark = stats_ref[own_ref[0], 4 * heads : 4 * heads + 8, :][passage : passage + 1]
            shares.append(jnp.exp(mark - best) / sum(jnp.exp(m - best) for m in marks))
        aux_ref[...] = jnp.concatenate(aux + shares + [jnp.zeros((4, 128), F32)], axis=0)

    for passage in range(2):
        norms = norm_ref[passage, pl.ds(pl.multiple_of(step * per_step, 8), per_step), :]
        dots = norm_ref[2 + passage, pl.ds(pl.multiple_of(step * per_step, 8), per_step), :]
        grads = []
        for head in range(per_step):
            scores, prob_grad, stacked = local_scores(
                kv_ref, qd_ref, head, passage, question_ref[passage], blocks_ref[passage]
            )
            probs = jnp.exp(scores - norms[head : head + 1])
            score_grad = probs * (prob_grad - dots[head : head + 1])
            left = jnp.concatenate([score_grad, probs], axis=1).astype(BF16)
            grad = jnp.dot(left, stacked, preferred_element_type=F32).astype(BF16)
            flat_ref[
                passage * SLOT : (passage + 1) * SLOT, head * 128 : (head + 1) * 128
            ] = grad
            grads.append(grad)
        grad_ref[passage * SLOT : (passage + 1) * SLOT] = jnp.swapaxes(
            jnp.stack(grads, axis=0), 0, 1
        )


def backward(own_question, own_blocks, enc_rank, order_row, key_value, gathered, stats):
    heads, tokens, pair_width = key_value.shape
    per_step = 8
    return pl.pallas_call(
        functools.partial(back_kernel, heads),
        grid_spec=pltpu.PrefetchScalarGridSpec(
            num_scalar_prefetch=4,
            grid=(heads // per_step,),
            in_specs=[
                pl.BlockSpec((per_step, tokens, pair_width), lambda i, *_: (i, 0, 0)),
                pl.BlockSpec((per_step,) + gathered.shape[1:], lambda i, *_: (i, 0, 0)),
                pl.BlockSpec(stats.shape, lambda i, *_: (0, 0, 0)),
            ],
            out_specs=[
                pl.BlockSpec((tokens, per_step, pair_width), lambda i, *_: (0, i, 0)),
                pl.BlockSpec((tokens, per_step * pair_width), lambda i, *_: (0, i)),
                pl.BlockSpec((8, 128), lambda i, *_: (0, 0)),
            ],
            scratch_shapes=[pltpu.VMEM((4, heads, 128), F32)],
        ),
        out_shape=[
            jax.ShapeDtypeStruct((tokens, heads, pair_width), BF16),
            jax.ShapeDtypeStruct((tokens, heads * pair_width), BF16),
            jax.ShapeDtypeStruct((8, 128), F32),
        ],
        compiler_params=pltpu.CompilerParams(vmem_limit_bytes=VMEM),
        cost_estimate=pl.CostEstimate(
            flops=3 << 30, bytes_accessed=10 << 20, transcendentals=1 << 20
        ),
        name="backward",
    )(own_question, own_blocks, enc_rank.reshape(1), order_row, key_value, gathered, stats)


def weight_kernel(which_ref, mine_ref, other_ref, own_ref, far_ref, o_ref):
    rows = SIDE * 128
    depth = mine_ref.shape[-1]
    near = mine_ref[...].reshape(rows, depth)
    far = other_ref[...].reshape(rows, depth)
    columns = own_ref.shape[1] // 2
    for half in range(2):
        at = slice(half * columns, (half + 1) * columns)
        total = jnp.dot(near, own_ref[:, at], preferred_element_type=F32)
        total += jnp.dot(far, far_ref[:, at], preferred_element_type=F32)
        o_ref[0, half] = total.astype(BF16)


def weight_chunks(which, part, mine, other, grad_own, grad_far):
    tokens = mine.shape[-1]
    columns = grad_own.shape[1] // 2
    count = which.shape[0]
    if part == 0:
        turned = pl.BlockSpec((1, SIDE, 128, tokens), lambda i, w: (w[i], 0, 0, 0))
    else:
        turned = pl.BlockSpec((SIDE, 1, 128, tokens), lambda i, w: (0, w[i], 0, 0))
    grads = pl.BlockSpec((tokens, columns), lambda i, w: (0, part))
    return pl.pallas_call(
        weight_kernel,
        grid_spec=pltpu.PrefetchScalarGridSpec(
            num_scalar_prefetch=1,
            grid=(count,),
            in_specs=[turned, turned, grads, grads],
            out_specs=pl.BlockSpec(
                (1, 2, SIDE * 128, columns // 2), lambda i, w: (i, 0, 0, 0)
            ),
        ),
        out_shape=jax.ShapeDtypeStruct((count, 2, SIDE * 128, columns // 2), BF16),
        compiler_params=pltpu.CompilerParams(vmem_limit_bytes=VMEM),
        cost_estimate=pl.CostEstimate(
            flops=count * 4 * SIDE * 128 * tokens * columns,
            bytes_accessed=count << 22,
            transcendentals=0,
        ),
        name="weight_chunks",
    )(which, mine, other, grad_own, grad_far)


def ring_pairs(axis, step):
    pairs = []
    for x in range(SIDE):
        for y in range(SIDE):
            to = ((x + step) % SIDE, y) if axis == 0 else (x, (y + step) % SIDE)
            pairs.append((x * SIDE + y, to[0] * SIDE + to[1]))
    return pairs


def send(value, axis, step):
    return lax.ppermute(value, "enc", ring_pairs(axis, step))


def add(*terms):
    return sum(t.astype(F32) for t in terms).astype(BF16)


def on_device(
    enc_states,
    kv_weight,
    queries,
    out_grad,
    passage_order,
    passage_blocks,
    ret_tokens,
    ret_weight,
    question_emb,
):
    pass_dev, _, slot_len, width = enc_states.shape
    heads, pair_width = kv_weight.shape[1:]
    question_count, query_len = queries.shape[:2]
    enc_rank = lax.axis_index("enc")
    dec_rank = lax.axis_index("dec")
    ret_rank = lax.axis_index("ret")
    order_row = passage_order[0]
    blocks_row = passage_blocks[0]
    tokens = pass_dev * slot_len
    swap = [(0, 1), (1, 0)]

    packed = jnp.concatenate(
        [queries[:, :, 0, :] * jnp.asarray(0.125, BF16), out_grad[:, :, 0, :]], axis=-1
    ).reshape(question_count * query_len, pair_width)
    gathered = lax.all_to_all(
        jnp.broadcast_to(packed[None], (N_ENC,) + packed.shape),
        "enc",
        split_axis=0,
        concat_axis=0,
        tiled=True,
    )

    tok_rows = enc_states.reshape(tokens, width)
    mine, to_send = turn(ret_rank, tok_rows)
    other = lax.ppermute(to_send, "ret", swap)
    key_value = project(tok_rows, kv_weight)

    own_pass = enc_rank * pass_dev + jnp.arange(pass_dev, dtype=jnp.int32)
    slot_of = jnp.sum(
        jnp.where(
            order_row[None, :] == own_pass[:, None],
            jnp.arange(order_row.shape[0], dtype=jnp.int32)[None, :],
            0,
        ),
        axis=1,
    )
    own_question = slot_of // PASS
    own_blocks = lax.dynamic_slice_in_dim(blocks_row, enc_rank * pass_dev, pass_dev)
    own_emb = jnp.sum(
        jnp.where(
            (own_question[:, None] == jnp.arange(question_count)[None, :])[..., None],
            question_emb[None],
            0.0,
        ),
        axis=1,
    )
    ret_rows = ret_tokens.reshape(tokens, ret_tokens.shape[3])
    ret_width = ret_rows.shape[1]
    pre_act = jnp.dot(ret_rows, ret_weight, preferred_element_type=F32).reshape(
        pass_dev, slot_len, ret_width
    )
    own_live = jnp.arange(slot_len, dtype=jnp.int32)[None, :] < BLK * own_blocks[:, None]
    own_length = (BLK * own_blocks).astype(F32)
    embed_own = (
        jnp.sum(jnp.where(own_live[..., None], jax.nn.gelu(pre_act), 0.0), axis=1)
        / own_length[:, None]
    )
    own_score = jnp.sum(own_emb * embed_own, axis=-1)
    score_rows = jnp.broadcast_to(
        jnp.concatenate([own_score, jnp.zeros((8 - pass_dev,), F32)])[:, None], (8, 128)
    )

    stats = local_stats(own_question, own_blocks, key_value, gathered, score_rows)
    stats_all = lax.all_to_all(
        jnp.broadcast_to(stats[None], (N_ENC,) + stats.shape),
        "enc",
        split_axis=0,
        concat_axis=0,
        tiled=True,
    )
    grad_rows, grad_flat, aux = backward(
        own_question, own_blocks, enc_rank, order_row, key_value, gathered, stats_all
    )
    kv_grad = grad_rows.reshape(pass_dev, 1, slot_len, heads, pair_width)
    grad_far = lax.ppermute(grad_flat, "ret", swap)

    mine4 = mine.reshape(SIDE, SIDE, 128, tokens)
    other4 = other.reshape(SIDE, SIDE, 128, tokens)
    at = (enc_rank // SIDE, enc_rank % SIDE)
    opposite, rest = [], []
    for part in range(2):
        which = (at[part] + jnp.array([2], jnp.int32)) % SIDE
        opposite.append(weight_chunks(which, part, mine4, other4, grad_flat, grad_far))
    came = []
    for part in range(2):
        came.append(
            (send(opposite[part][0, 0], part, 1), send(opposite[part][0, 1], part, -1))
        )
    for part in range(2):
        which = (at[part] + jnp.array([1, 3, 0], jnp.int32)) % SIDE
        rest.append(weight_chunks(which, part, mine4, other4, grad_flat, grad_far))
    sent = []
    for part in range(2):
        chunk = rest[part]
        up = jnp.stack([add(chunk[0, 0], came[part][0]), chunk[0, 1]])
        down = jnp.stack([chunk[1, 0], add(chunk[1, 1], came[part][1])])
        sent.append((send(up, part, 1), send(down, part, -1)))
    sums = []
    for part in range(2):
        total = add(rest[part][2], sent[part][0], sent[part][1])
        sums.append(total.reshape(2, SIDE, 128, total.shape[-1]))
    pick = lambda a, k: lax.dynamic_index_in_dim(a, k % SIDE, 1, keepdims=False)
    came = []
    for part in range(2):
        far = pick(sums[part], at[1 - part] + 2)
        came.append((send(far[0], 1 - part, 1), send(far[1], 1 - part, -1)))
    sent = []
    for part in range(2):
        up, down = pick(sums[part], at[1 - part] + 1), pick(sums[part], at[1 - part] + 3)
        up = jnp.stack([add(up[0], came[part][0]), up[1]])
        down = jnp.stack([down[0], add(down[1], came[part][1])])
        sent.append((send(up, 1 - part, 1), send(down, 1 - part, -1)))
    done = []
    for part in range(2):
        total = add(pick(sums[part], at[1 - part]), sent[part][0], sent[part][1])
        done += [total[0], total[1]]
    weight_total = jnp.concatenate(done, axis=1).reshape(128, heads, pair_width)

    masses = aux
    for step in range(1, N_DEC):
        masses = masses + lax.ppermute(
            aux, "dec", [(i, (i + step) % N_DEC) for i in range(N_DEC)]
        )
    own_mass = masses[:pass_dev, 0] / (N_DEC * heads * query_len)
    gap = aux[pass_dev : 2 * pass_dev, 0] - own_mass
    embed_grad = gap[:, None] * own_emb / own_length[:, None]
    hidden_grad = jnp.where(own_live[..., None], embed_grad[:, None, :], 0.0)
    pre_grad = gelu_grad(pre_act, hidden_grad).astype(BF16).reshape(tokens, ret_width)
    share = ret_width // N_DEC
    part_rows = lax.dynamic_slice_in_dim(ret_rows, dec_rank * share, share, axis=1)
    ret_part = lax.dot_general(
        part_rows, pre_grad, (((0,), (0,)), ((), ())), preferred_element_type=F32
    ).reshape(2, share // 2, ret_width)
    keep = lax.dynamic_index_in_dim(ret_part, ret_rank, 0, keepdims=False)
    give = lax.dynamic_index_in_dim(ret_part, 1 - ret_rank, 0, keepdims=False)
    ret_half = add(keep, lax.ppermute(give.astype(BF16), "ret", swap))
    pieces = lax.all_to_all(
        ret_half.reshape(N_ENC, share // 2 // N_ENC * ret_width),
        "enc",
        split_axis=0,
        concat_axis=0,
        tiled=True,
    )
    piece = jnp.sum(pieces.astype(F32), axis=0, keepdims=True).astype(BF16)
    half = lax.all_to_all(
        jnp.broadcast_to(piece, pieces.shape), "enc", split_axis=0, concat_axis=0, tiled=True
    ).reshape(share // 2, ret_width)
    half_far = lax.ppermute(half, "ret", swap)
    quarter = jnp.where(
        ret_rank == 0, jnp.stack([half, half_far]), jnp.stack([half_far, half])
    ).reshape(share, ret_width)
    ret_weight_grad = jnp.zeros((N_DEC, share, ret_width), BF16)
    for step in range(N_DEC):
        piece = quarter
        if step:
            piece = lax.ppermute(
                quarter, "dec", [(i, (i + step) % N_DEC) for i in range(N_DEC)]
            )
        ret_weight_grad = lax.dynamic_update_index_in_dim(
            ret_weight_grad, piece, (dec_rank - step) % N_DEC, 0
        )
    return (kv_grad, weight_total, ret_weight_grad.reshape(ret_width, ret_width))


def solution(mesh):
    return jax.shard_map(
        on_device,
        mesh=mesh,
        in_specs=(
            P("enc", "ret", None, None),
            P(None, "dec", None),
            P("ret", None, ("dec", "enc"), None),
            P("ret", None, ("dec", "enc"), None),
            P("ret", None),
            P("ret", None),
            P("enc", "ret", None, None),
            P(),
            P("ret", None),
        ),
        out_specs=(P("enc", "ret", None, "dec", None), P(("enc", "ret"), "dec", None), P()),
        check_vma=False,
    )
```

```python
import functools

import jax
import jax.numpy as jnp
from jax import lax
from jax.experimental import pallas as pl
from jax.experimental.pallas import tpu as pltpu
from jax.sharding import PartitionSpec as P

BLK = 128
PASS = 8
N_ENC = 16
SIDE = 4
N_DEC = 4
LQ = 128
HD = 64
SLOT = 256
F32 = jnp.float32
BF16 = jnp.bfloat16
VMEM = 60 << 20


def gelu_grad(pre_act, upstream):
    return jax.vjp(jax.nn.gelu, pre_act)[1](upstream)[0]


def project_kernel(x_ref, w_ref, o_ref):
    @pl.when(pl.program_id(0) == 0)
    def _():
        o_ref[...] = jnp.zeros_like(o_ref)

    rows = x_ref[...]
    by_head = jnp.swapaxes(w_ref[...], 0, 1)
    for pair in range(by_head.shape[0] // 2):
        both = jnp.concatenate([by_head[2 * pair], by_head[2 * pair + 1]], axis=1)
        part = jnp.dot(rows, both, preferred_element_type=F32)
        o_ref[2 * pair] += part[:, :128]
        o_ref[2 * pair + 1] += part[:, 128:]


def project(tok_rows, kv_weight, depth=512):
    tokens, width = tok_rows.shape
    heads, pair_width = kv_weight.shape[1:]
    return pl.pallas_call(
        project_kernel,
        grid=(width // depth,),
        out_shape=jax.ShapeDtypeStruct((heads, tokens, pair_width), F32),
        in_specs=[
            pl.BlockSpec((tokens, depth), lambda i: (0, i)),
            pl.BlockSpec((depth, heads, pair_width), lambda i: (i, 0, 0)),
        ],
        out_specs=pl.BlockSpec((heads, tokens, pair_width), lambda i: (0, 0, 0)),
        compiler_params=pltpu.CompilerParams(vmem_limit_bytes=VMEM),
        cost_estimate=pl.CostEstimate(
            flops=2 * tokens * width * heads * pair_width,
            bytes_accessed=24 << 20,
            transcendentals=0,
        ),
        name="project",
    )(tok_rows, kv_weight)


def turn_kernel(rank_ref, x_ref, mine_ref, send_ref):
    first = rank_ref[0] == 0
    for block in range(mine_ref.shape[0]):
        even = x_ref[:, block * 256 : block * 256 + 128].T
        odd = x_ref[:, block * 256 + 128 : block * 256 + 256].T
        mine_ref[block] = jnp.where(first, even, odd)
        send_ref[block] = jnp.where(first, odd, even)


def turn(ret_rank, tok_rows, per_step=8):
    tokens, width = tok_rows.shape
    half = jax.ShapeDtypeStruct((N_ENC, 128, tokens), BF16)
    return pl.pallas_call(
        turn_kernel,
        grid_spec=pltpu.PrefetchScalarGridSpec(
            num_scalar_prefetch=1,
            grid=(N_ENC // per_step,),
            in_specs=[pl.BlockSpec((tokens, 256 * per_step), lambda i, r: (0, i))],
            out_specs=[pl.BlockSpec((per_step, 128, tokens), lambda i, r: (i, 0, 0))] * 2,
        ),
        out_shape=[half, half],
        compiler_params=pltpu.CompilerParams(vmem_limit_bytes=VMEM),
        cost_estimate=pl.CostEstimate(flops=0, bytes_accessed=12 << 20, transcendentals=0),
        name="turn",
    )(ret_rank.reshape(1), tok_rows)


def local_scores(kv_ref, qd_ref, head, passage, question, blocks):
    pair = kv_ref[head, passage * SLOT : (passage + 1) * SLOT, :]
    high = pair.astype(BF16)
    low = (pair - high.astype(F32)).astype(BF16)
    rows = qd_ref[head, pl.ds(pl.multiple_of(question * LQ, LQ), LQ), :]
    lane = lax.broadcasted_iota(jnp.int32, rows.shape, 1)
    zero = jnp.zeros_like(rows)
    stacked = jnp.concatenate(
        [jnp.where(lane < HD, rows, zero), jnp.where(lane < HD, zero, rows)], axis=0
    )
    both = lax.dot_general(
        jnp.concatenate([high, low], axis=1),
        jnp.concatenate([stacked, stacked], axis=1),
        (((1,), (1,)), ((), ())),
        preferred_element_type=F32,
    )
    scores = both[:, :LQ]
    place = lax.broadcasted_iota(jnp.int32, scores.shape, 0)
    return jnp.where(place < BLK * blocks, scores, -1e30), both[:, LQ:], stacked


def stats_kernel(heads, question_ref, blocks_ref, kv_ref, qd_ref, score_ref, o_ref, rows_ref):
    step = pl.program_id(0)
    per_step = kv_ref.shape[0]
    for passage in range(2):
        tops, dots = [], []
        for head in range(per_step):
            scores, prob_grad, _ = local_scores(
                kv_ref, qd_ref, head, passage, question_ref[passage], blocks_ref[passage]
            )
            top = jnp.max(scores, axis=0, keepdims=True)
            expo = jnp.exp(scores - top)
            total = jnp.sum(expo, axis=0, keepdims=True)
            tops.append(top + jnp.log(total))
            dots.append(jnp.sum(expo * prob_grad, axis=0, keepdims=True) / total)
        place = passage * heads + step * per_step
        rows_ref[pl.ds(pl.multiple_of(place, 8), per_step), :] = jnp.concatenate(tops, axis=0)
        rows_ref[pl.ds(pl.multiple_of(2 * heads + place, 8), per_step), :] = jnp.concatenate(
            dots, axis=0
        )

    @pl.when(step == pl.num_programs(0) - 1)
    def _():
        rows_ref[4 * heads :, :] = score_ref[...]
        o_ref[...] = jnp.broadcast_to(rows_ref[...][None], o_ref.shape)


def local_stats(own_question, own_blocks, key_value, gathered, score_rows):
    heads, tokens, pair_width = key_value.shape
    per_step = 8
    rows = 4 * heads + 8
    return pl.pallas_call(
        functools.partial(stats_kernel, heads),
        grid_spec=pltpu.PrefetchScalarGridSpec(
            num_scalar_prefetch=2,
            grid=(heads // per_step,),
            in_specs=[
                pl.BlockSpec((per_step, tokens, pair_width), lambda i, *_: (i, 0, 0)),
                pl.BlockSpec((per_step,) + gathered.shape[1:], lambda i, *_: (i, 0, 0)),
                pl.BlockSpec((8, 128), lambda i, *_: (0, 0)),
            ],
            out_specs=pl.BlockSpec((N_ENC, rows, 128), lambda i, *_: (0, 0, 0)),
            scratch_shapes=[pltpu.VMEM((rows, 128), F32)],
        ),
        out_shape=jax.ShapeDtypeStruct((N_ENC, rows, 128), F32),
        compiler_params=pltpu.CompilerParams(vmem_limit_bytes=VMEM),
        cost_estimate=pl.CostEstimate(
            flops=2 << 30, bytes_accessed=6 << 20, transcendentals=1 << 20
        ),
        name="local_stats",
    )(own_question, own_blocks, key_value, gathered, score_rows)


def merge_stats(heads, question_ref, own_ref, order_ref, stats_ref, norm_ref, aux_ref):
    masses, shares = [], []
    for passage in range(2):
        tops, dots, marks = [], [], []
        for slot in range(PASS):
            place = order_ref[question_ref[passage] * PASS + slot]
            owner = place // 2
            at = place - 2 * owner
            tops.append(stats_ref[owner, pl.ds(pl.multiple_of(at * heads, heads), heads), :])
            dots.append(
                stats_ref[owner, pl.ds(pl.multiple_of((2 + at) * heads, heads), heads), :]
            )
            pair = stats_ref[owner, 4 * heads : 4 * heads + 8, :]
            marks.append(jnp.where(at == 0, pair[0:1], pair[1:2]))
        top = functools.reduce(jnp.maximum, tops)
        norm = top + jnp.log(sum(jnp.exp(t - top) for t in tops))
        norm_ref[passage] = norm
        norm_ref[2 + passage] = sum(jnp.exp(t - norm) * d for t, d in zip(tops, dots))
        own = stats_ref[own_ref[0], passage * heads : (passage + 1) * heads, :]
        mass = jnp.sum(jnp.exp(own - norm), axis=0, keepdims=True)
        masses.append(jnp.broadcast_to(jnp.sum(mass, axis=1, keepdims=True), (1, 128)))
        best = functools.reduce(jnp.maximum, marks)
        mark = stats_ref[own_ref[0], 4 * heads : 4 * heads + 8, :][passage : passage + 1]
        shares.append(jnp.exp(mark - best) / sum(jnp.exp(m - best) for m in marks))
    aux_ref[...] = jnp.concatenate(masses + shares + [jnp.zeros((4, 128), F32)], axis=0)


def back_heads(part, question_ref, blocks_ref, kv_ref, qd_ref, norm_ref, flat_ref):
    per_step = kv_ref.shape[0]
    first = part * 8 + pl.program_id(0) * per_step
    for passage in range(2):
        for head in range(per_step):
            scores, prob_grad, stacked = local_scores(
                kv_ref, qd_ref, head, passage, question_ref[passage], blocks_ref[passage]
            )
            norm = norm_ref[passage, pl.ds(first + head, 1), :]
            dot = norm_ref[2 + passage, pl.ds(first + head, 1), :]
            probs = jnp.exp(scores - norm)
            score_grad = probs * (prob_grad - dot)
            left = jnp.concatenate([score_grad, probs], axis=1).astype(BF16)
            grad = jnp.dot(left, stacked, preferred_element_type=F32).astype(BF16)
            flat_ref[
                passage * SLOT : (passage + 1) * SLOT, head * 128 : (head + 1) * 128
            ] = grad


def back_first_kernel(
    heads, question_ref, blocks_ref, own_ref, order_ref, kv_ref, qd_ref, stats_ref, flat_ref, norm_ref, aux_ref
):
    @pl.when(pl.program_id(0) == 0)
    def _():
        merge_stats(heads, question_ref, own_ref, order_ref, stats_ref, norm_ref, aux_ref)

    back_heads(0, question_ref, blocks_ref, kv_ref, qd_ref, norm_ref, flat_ref)


def back_second_kernel(question_ref, blocks_ref, kv_ref, qd_ref, norm_ref, flat_ref):
    back_heads(1, question_ref, blocks_ref, kv_ref, qd_ref, norm_ref, flat_ref)


BACK_COST = pl.CostEstimate(flops=3 << 29, bytes_accessed=5 << 20, transcendentals=1 << 19)


def back_specs(key_value, gathered, part, per_step):
    base = part * 8 // per_step
    tokens, pair_width = key_value.shape[1:]
    return [
        pl.BlockSpec((per_step, tokens, pair_width), lambda i, *_: (base + i, 0, 0)),
        pl.BlockSpec((per_step,) + gathered.shape[1:], lambda i, *_: (base + i, 0, 0)),
    ]


def back_first(own_question, own_blocks, enc_rank, order_row, key_value, gathered, stats, per_step=4):
    heads, tokens, pair_width = key_value.shape
    return pl.pallas_call(
        functools.partial(back_first_kernel, heads),
        grid_spec=pltpu.PrefetchScalarGridSpec(
            num_scalar_prefetch=4,
            grid=(8 // per_step,),
            in_specs=back_specs(key_value, gathered, 0, per_step)
            + [pl.BlockSpec(stats.shape, lambda i, *_: (0, 0, 0))],
            out_specs=[
                pl.BlockSpec((tokens, per_step * pair_width), lambda i, *_: (0, i)),
                pl.BlockSpec((4, heads, 128), lambda i, *_: (0, 0, 0)),
                pl.BlockSpec((8, 128), lambda i, *_: (0, 0)),
            ],
        ),
        out_shape=[
            jax.ShapeDtypeStruct((tokens, 8 * pair_width), BF16),
            jax.ShapeDtypeStruct((4, heads, 128), F32),
            jax.ShapeDtypeStruct((8, 128), F32),
        ],
        compiler_params=pltpu.CompilerParams(vmem_limit_bytes=VMEM),
        cost_estimate=BACK_COST,
        name="back_first",
    )(own_question, own_blocks, enc_rank.reshape(1), order_row, key_value, gathered, stats)


def back_second(own_question, own_blocks, key_value, gathered, norms, per_step=4):
    heads, tokens, pair_width = key_value.shape
    return pl.pallas_call(
        back_second_kernel,
        grid_spec=pltpu.PrefetchScalarGridSpec(
            num_scalar_prefetch=2,
            grid=(8 // per_step,),
            in_specs=back_specs(key_value, gathered, 1, per_step)
            + [pl.BlockSpec(norms.shape, lambda i, *_: (0, 0, 0))],
            out_specs=pl.BlockSpec((tokens, per_step * pair_width), lambda i, *_: (0, i)),
        ),
        out_shape=jax.ShapeDtypeStruct((tokens, 8 * pair_width), BF16),
        compiler_params=pltpu.CompilerParams(vmem_limit_bytes=VMEM),
        cost_estimate=BACK_COST,
        name="back_second",
    )(own_question, own_blocks, key_value, gathered, norms)


def product(near_ref, far_ref, own_ref, other_ref):
    rows, depth = SIDE * 128, near_ref.shape[-1]
    total = jnp.dot(near_ref[...].reshape(rows, depth), own_ref[...], preferred_element_type=F32)
    return total + jnp.dot(
        far_ref[...].reshape(rows, depth), other_ref[...], preferred_element_type=F32
    )


def chunk_spec(part, tokens, which):
    if part == 0:
        return pl.BlockSpec((1, SIDE, 128, tokens), lambda i, w: (w[which], 0, 0, 0))
    return pl.BlockSpec((SIDE, 1, 128, tokens), lambda i, w: (0, w[which], 0, 0))


def chunk_call(kernel, name, which, part, turned, grads, extra, extra_specs, out_specs, out_shape):
    tokens, columns = grads[0].shape
    half = pl.BlockSpec((tokens, columns // 2), lambda i, w: (0, i))
    chunks = which.shape[0]
    turned_specs, turned_args = [], []
    for index in range(chunks):
        turned_specs += [chunk_spec(part, tokens, index)] * 2
        turned_args += turned
    return pl.pallas_call(
        kernel,
        grid_spec=pltpu.PrefetchScalarGridSpec(
            num_scalar_prefetch=1,
            grid=(2,),
            in_specs=turned_specs + [half, half] + extra_specs,
            out_specs=out_specs,
        ),
        out_shape=out_shape,
        compiler_params=pltpu.CompilerParams(vmem_limit_bytes=VMEM),
        cost_estimate=pl.CostEstimate(
            flops=chunks * 4 * SIDE * 128 * tokens * columns,
            bytes_accessed=(2 * chunks + 4) << 20,
            transcendentals=0,
        ),
        name=name,
    )(which, *turned_args, *grads, *extra)


def far_kernel(which_ref, near_ref, far_ref, own_ref, other_ref, note_ref, a_ref, b_ref, out_ref):
    total = product(near_ref, far_ref, own_ref, other_ref).astype(BF16)

    @pl.when(pl.program_id(0) == 0)
    def _():
        a_ref[...] = total
        out_ref[...] = note_ref[...]

    @pl.when(pl.program_id(0) == 1)
    def _():
        b_ref[...] = total


def far_chunk(which, part, turned, grads, note):
    rows, columns = SIDE * 128, grads[0].shape[1] // 2
    half = jax.ShapeDtypeStruct((rows, columns), BF16)
    note_spec = pl.BlockSpec((8, 128), lambda i, w: (0, 0))
    half_spec = pl.BlockSpec((rows, columns), lambda i, w: (0, 0))
    return chunk_call(
        far_kernel,
        "far_chunk",
        which,
        part,
        turned,
        grads,
        [note],
        [note_spec],
        [half_spec, half_spec, note_spec],
        [half, half, jax.ShapeDtypeStruct((8, 128), F32)],
    )


def own_kernel(which_ref, near_ref, far_ref, own_ref, other_ref, o_ref):
    o_ref[0] = product(near_ref, far_ref, own_ref, other_ref).astype(BF16)


def own_chunk(which, part, turned, grads):
    rows, columns = SIDE * 128, grads[0].shape[1] // 2
    return chunk_call(
        own_kernel,
        "own_chunk",
        which,
        part,
        turned,
        grads,
        [],
        [],
        pl.BlockSpec((1, rows, columns), lambda i, w: (i, 0, 0)),
        jax.ShapeDtypeStruct((2, rows, columns), BF16),
    )


def side_kernel(
    which_ref, up_near, up_far, down_near, down_far, own_ref, other_ref, a_ref, b_ref, up_ref, down_ref
):
    first = pl.program_id(0) == 0
    zero = jnp.zeros(a_ref.shape, F32)
    up = product(up_near, up_far, own_ref, other_ref)
    up_ref[0] = (up + jnp.where(first, a_ref[...].astype(F32), zero)).astype(BF16)
    down = product(down_near, down_far, own_ref, other_ref)
    down_ref[0] = (down + jnp.where(first, zero, b_ref[...].astype(F32))).astype(BF16)


def side_chunks(which, part, turned, grads, came):
    rows, columns = SIDE * 128, grads[0].shape[1] // 2
    both = jax.ShapeDtypeStruct((2, rows, columns), BF16)
    out = pl.BlockSpec((1, rows, columns), lambda i, w: (i, 0, 0))
    full = pl.BlockSpec((rows, columns), lambda i, w: (0, 0))
    return chunk_call(
        side_kernel, "side_chunks", which, part, turned, grads, list(came), [full, full], [out, out], [both, both]
    )


def total_kernel(which_ref, own_ref, up_ref, down_ref, *out_refs):
    total = own_ref[...].astype(F32) + up_ref[...].astype(F32) + down_ref[...].astype(F32)
    for step, ref in enumerate(out_refs):

        @pl.when(pl.program_id(0) == step)
        def _():
            ref[...] = total[:, 0].astype(BF16)


def totals(first, own, up, down):
    columns = own.shape[-1]
    cut = lambda a: a.reshape(2, SIDE, 128, columns)
    block = pl.BlockSpec((2, 1, 128, columns), lambda i, w: (0, (w[0] + i) % SIDE, 0, 0))
    out = pl.BlockSpec((2, 128, columns), lambda i, w: (0, 0, 0))
    return pl.pallas_call(
        total_kernel,
        grid_spec=pltpu.PrefetchScalarGridSpec(
            num_scalar_prefetch=1, grid=(SIDE,), in_specs=[block] * 3, out_specs=[out] * SIDE
        ),
        out_shape=[jax.ShapeDtypeStruct((2, 128, columns), BF16)] * SIDE,
        compiler_params=pltpu.CompilerParams(vmem_limit_bytes=VMEM),
        cost_estimate=pl.CostEstimate(flops=2 << 20, bytes_accessed=4 << 20, transcendentals=0),
        name="totals",
    )(first.reshape(1), cut(own), cut(up), cut(down))


def finish_kernel(*refs):
    pieces, out_ref = refs[:-1], refs[-1]
    heads = []
    for part in range(2):
        total = sum(r[...].astype(F32) for r in pieces[part * SIDE : (part + 1) * SIDE])
        total = total.astype(BF16)
        for half in range(2):
            for head in range(4):
                heads.append(total[half, :, head * 128 : (head + 1) * 128])
    out_ref[...] = jnp.swapaxes(jnp.stack(heads), 0, 1)


def finish(pieces):
    return pl.pallas_call(
        finish_kernel,
        out_shape=jax.ShapeDtypeStruct((128, 16, 128), BF16),
        compiler_params=pltpu.CompilerParams(vmem_limit_bytes=VMEM),
        name="finish",
    )(*pieces)


def by_token_kernel(a_ref, b_ref, o_ref):
    heads = [ref[:, h * 128 : (h + 1) * 128] for ref in (a_ref, b_ref) for h in range(8)]
    o_ref[...] = jnp.swapaxes(jnp.stack(heads), 0, 1)


def by_token(a, b, rows=128):
    tokens, columns = a.shape
    block = pl.BlockSpec((rows, columns), lambda i: (i, 0))
    return pl.pallas_call(
        by_token_kernel,
        grid=(tokens // rows,),
        in_specs=[block, block],
        out_specs=pl.BlockSpec((rows, 16, 128), lambda i: (i, 0, 0)),
        out_shape=jax.ShapeDtypeStruct((tokens, 16, 128), BF16),
        compiler_params=pltpu.CompilerParams(vmem_limit_bytes=VMEM),
        cost_estimate=pl.CostEstimate(flops=0, bytes_accessed=6 << 20, transcendentals=0),
        name="by_token",
    )(a, b)


def gap_kernel(heads_rows, rank_ref, aux_ref, m1_ref, m2_ref, m3_ref, part_ref, gate_ref, keep_ref, give_ref):
    rows = keep_ref.shape[0]
    mass = (aux_ref[0:2] + m1_ref[0:2]) + (m2_ref[0:2] + m3_ref[0:2])
    gap = aux_ref[2:4] - mass / heads_rows
    rank = rank_ref[0]

    def at(place):
        here = pl.ds(pl.multiple_of(place * rows, 8), rows)
        return gap[0:1, 0:1] * part_ref[0, here, :] + gap[1:2, 0:1] * part_ref[1, here, :]

    keep_ref[...] = at(rank)
    give_ref[...] = at(1 - rank).astype(BF16)


def apply_gap(ret_rank, aux, masses, parts, heads_rows, gate):
    _, rows, columns = parts.shape
    whole = lambda *shape: pl.BlockSpec(shape, lambda i, r: (0,) * len(shape))
    return pl.pallas_call(
        functools.partial(gap_kernel, float(heads_rows)),
        grid_spec=pltpu.PrefetchScalarGridSpec(
            num_scalar_prefetch=1,
            grid=(1,),
            in_specs=[whole(8, 128)] * 4
            + [whole(2, rows, columns), pl.BlockSpec(memory_space=pl.ANY)],
            out_specs=[whole(rows // 2, columns)] * 2,
        ),
        out_shape=[
            jax.ShapeDtypeStruct((rows // 2, columns), F32),
            jax.ShapeDtypeStruct((rows // 2, columns), BF16),
        ],
        compiler_params=pltpu.CompilerParams(vmem_limit_bytes=VMEM),
        cost_estimate=pl.CostEstimate(flops=1 << 19, bytes_accessed=2 << 20, transcendentals=0),
        name="apply_gap",
    )(ret_rank.reshape(1), aux, *masses, parts, gate)


def ring_pairs(axis, step):
    pairs = []
    for x in range(SIDE):
        for y in range(SIDE):
            to = ((x + step) % SIDE, y) if axis == 0 else (x, (y + step) % SIDE)
            pairs.append((x * SIDE + y, to[0] * SIDE + to[1]))
    return pairs


def send(value, axis, step):
    return lax.ppermute(value, "enc", ring_pairs(axis, step))


def add(*terms):
    return sum(t.astype(F32) for t in terms).astype(BF16)


def on_device(
    enc_states,
    kv_weight,
    queries,
    out_grad,
    passage_order,
    passage_blocks,
    ret_tokens,
    ret_weight,
    question_emb,
):
    pass_dev, _, slot_len, width = enc_states.shape
    heads, pair_width = kv_weight.shape[1:]
    question_count, query_len = queries.shape[:2]
    enc_rank = lax.axis_index("enc")
    dec_rank = lax.axis_index("dec")
    ret_rank = lax.axis_index("ret")
    order_row = passage_order[0]
    blocks_row = passage_blocks[0]
    tokens = pass_dev * slot_len
    swap = [(0, 1), (1, 0)]

    packed = jnp.concatenate(
        [queries[:, :, 0, :] * jnp.asarray(0.125, BF16), out_grad[:, :, 0, :]], axis=-1
    ).reshape(question_count * query_len, pair_width)
    gathered = lax.all_to_all(
        jnp.broadcast_to(packed[None], (N_ENC,) + packed.shape),
        "enc",
        split_axis=0,
        concat_axis=0,
        tiled=True,
    )

    tok_rows = enc_states.reshape(tokens, width)
    mine, to_send = turn(ret_rank, tok_rows)
    other = lax.ppermute(to_send, "ret", swap)
    key_value = project(tok_rows, kv_weight)

    own_pass = enc_rank * pass_dev + jnp.arange(pass_dev, dtype=jnp.int32)
    slot_of = jnp.sum(
        jnp.where(
            order_row[None, :] == own_pass[:, None],
            jnp.arange(order_row.shape[0], dtype=jnp.int32)[None, :],
            0,
        ),
        axis=1,
    )
    own_question = slot_of // PASS
    own_blocks = lax.dynamic_slice_in_dim(blocks_row, enc_rank * pass_dev, pass_dev)
    own_emb = jnp.sum(
        jnp.where(
            (own_question[:, None] == jnp.arange(question_count)[None, :])[..., None],
            question_emb[None],
            0.0,
        ),
        axis=1,
    )
    ret_rows = ret_tokens.reshape(tokens, ret_tokens.shape[3])
    ret_width = ret_rows.shape[1]
    pre_act = jnp.dot(ret_rows, ret_weight, preferred_element_type=F32).reshape(
        pass_dev, slot_len, ret_width
    )
    own_live = jnp.arange(slot_len, dtype=jnp.int32)[None, :] < BLK * own_blocks[:, None]
    own_length = (BLK * own_blocks).astype(F32)
    embed_own = (
        jnp.sum(jnp.where(own_live[..., None], jax.nn.gelu(pre_act), 0.0), axis=1)
        / own_length[:, None]
    )
    own_score = jnp.sum(own_emb * embed_own, axis=-1)
    score_rows = jnp.broadcast_to(
        jnp.concatenate([own_score, jnp.zeros((8 - pass_dev,), F32)])[:, None], (8, 128)
    )

    hidden_grad = jnp.where(
        own_live[..., None], (own_emb / own_length[:, None])[:, None, :], 0.0
    )
    pre_grad = gelu_grad(pre_act, hidden_grad).astype(BF16)
    share = ret_width // N_DEC
    part_rows = lax.dynamic_slice_in_dim(ret_rows, dec_rank * share, share, axis=1)
    ret_parts = lax.dot_general(
        part_rows.reshape(pass_dev, slot_len, share),
        pre_grad,
        (((1,), (1,)), ((0,), (0,))),
        preferred_element_type=F32,
    )

    stats = local_stats(own_question, own_blocks, key_value, gathered, score_rows)
    stats_all = lax.all_to_all(stats, "enc", split_axis=0, concat_axis=0, tiled=True)
    flat_a, norms, aux = back_first(
        own_question, own_blocks, enc_rank, order_row, key_value, gathered, stats_all
    )
    far_a = lax.ppermute(flat_a, "ret", swap)
    flat_b = back_second(own_question, own_blocks, key_value, gathered, norms)
    far_b = lax.ppermute(flat_b, "ret", swap)

    turned = [
        mine.reshape(SIDE, SIDE, 128, tokens),
        other.reshape(SIDE, SIDE, 128, tokens),
    ]
    grads = [[flat_a, far_a], [flat_b, far_b]]
    at = (enc_rank // SIDE, enc_rank % SIDE)
    steps = lambda part, *ks: (at[part] + jnp.array(ks, jnp.int32)) % SIDE
    came = []
    for part in range(2):
        a, b, aux = far_chunk(steps(part, 2), part, turned, grads[part], aux)
        came.append((send(a, part, 1), send(b, part, -1)))
    sent = []
    for part in range(2):
        up, down = side_chunks(steps(part, 1, 3), part, turned, grads[part], came[part])
        sent.append((send(up, part, 1), send(down, part, -1)))
    gate = up
    own = [own_chunk(steps(part, 0), part, turned, grads[part]) for part in range(2)]
    pieces = []
    for part in range(2):
        cuts = totals(at[1 - part], own[part], *sent[part])
        pieces.append(cuts[0])
        pieces += [send(cuts[k], 1 - part, k) for k in range(1, SIDE)]
    weight_total = finish(pieces)
    kv_grad = by_token(flat_a, flat_b).reshape(pass_dev, 1, slot_len, heads, pair_width)

    masses = [
        lax.ppermute(aux, "dec", [(i, (i + step) % N_DEC) for i in range(N_DEC)])
        for step in range(1, N_DEC)
    ]
    keep, give = apply_gap(
        ret_rank, aux, masses, ret_parts, N_DEC * heads * query_len, gate
    )
    ret_half = add(keep, lax.ppermute(give, "ret", swap))
    pieces = lax.all_to_all(
        ret_half.reshape(N_ENC, share // 2 // N_ENC * ret_width),
        "enc",
        split_axis=0,
        concat_axis=0,
        tiled=True,
    )
    piece = jnp.sum(pieces.astype(F32), axis=0, keepdims=True).astype(BF16)
    half = lax.all_to_all(
        jnp.broadcast_to(piece, pieces.shape), "enc", split_axis=0, concat_axis=0, tiled=True
    ).reshape(share // 2, ret_width)
    half_far = lax.ppermute(half, "ret", swap)
    quarter = jnp.where(
        ret_rank == 0, jnp.stack([half, half_far]), jnp.stack([half_far, half])
    ).reshape(share, ret_width)
    ret_weight_grad = jnp.zeros((N_DEC, share, ret_width), BF16)
    for step in range(N_DEC):
        piece = quarter
        if step:
            piece = lax.ppermute(
                quarter, "dec", [(i, (i + step) % N_DEC) for i in range(N_DEC)]
            )
        ret_weight_grad = lax.dynamic_update_index_in_dim(
            ret_weight_grad, piece, (dec_rank - step) % N_DEC, 0
        )
    return (kv_grad, weight_total, ret_weight_grad.reshape(ret_width, ret_width))


def solution(mesh):
    return jax.shard_map(
        on_device,
        mesh=mesh,
        in_specs=(
            P("enc", "ret", None, None),
            P(None, "dec", None),
            P("ret", None, ("dec", "enc"), None),
            P("ret", None, ("dec", "enc"), None),
            P("ret", None),
            P("ret", None),
            P("enc", "ret", None, None),
            P(),
            P("ret", None),
        ),
        out_specs=(P("enc", "ret", None, "dec", None), P(("enc", "ret"), "dec", None), P()),
        check_vma=False,
    )
```

```python
import functools

import jax
import jax.numpy as jnp
from jax import lax
from jax.experimental import pallas as pl
from jax.experimental.pallas import tpu as pltpu
from jax.sharding import PartitionSpec as P

BLK = 128
PASS = 8
N_ENC = 16
SIDE = 4
N_DEC = 4
LQ = 128
HD = 64
SLOT = 256
F32 = jnp.float32
BF16 = jnp.bfloat16
VMEM = 60 << 20


def small_cost():
    return pl.CostEstimate(flops=1 << 10, bytes_accessed=1 << 10, transcendentals=0)


def gelu_grad(pre_act, upstream):
    return jax.vjp(jax.nn.gelu, pre_act)[1](upstream)[0]


def pack_kernel(order_ref, q_ref, d_ref, o_ref):
    rows = o_ref.shape[1]
    packed = []
    for question in range(q_ref.shape[0] // rows):
        at = slice(question * rows, (question + 1) * rows)
        packed.append(
            jnp.concatenate([q_ref[at] * jnp.asarray(0.125, BF16), d_ref[at]], axis=1)
        )
    for slot in range(o_ref.shape[0]):
        o_ref[order_ref[slot]] = packed[slot // PASS]


def pack(order_row, q_rows, d_rows):
    total, head_dim = q_rows.shape
    passages = order_row.shape[0]
    return pl.pallas_call(
        pack_kernel,
        grid_spec=pltpu.PrefetchScalarGridSpec(
            num_scalar_prefetch=1,
            grid=(1,),
            in_specs=[pl.BlockSpec((total, head_dim), lambda i, o: (0, 0))] * 2,
            out_specs=pl.BlockSpec((passages, LQ, 2 * head_dim), lambda i, o: (0, 0, 0)),
        ),
        out_shape=jax.ShapeDtypeStruct((passages, LQ, 2 * head_dim), BF16),
        compiler_params=pltpu.CompilerParams(vmem_limit_bytes=VMEM),
        cost_estimate=small_cost(),
        name="pack",
    )(order_row, q_rows, d_rows)


def project_kernel(x_ref, w_ref, o_ref):
    @pl.when(pl.program_id(0) == 0)
    def _():
        o_ref[...] = jnp.zeros_like(o_ref)

    rows = x_ref[...]
    by_head = jnp.swapaxes(w_ref[...], 0, 1)
    for pair in range(by_head.shape[0] // 2):
        both = jnp.concatenate([by_head[2 * pair], by_head[2 * pair + 1]], axis=1)
        part = jnp.dot(rows, both, preferred_element_type=F32)
        o_ref[2 * pair] += part[:, :128]
        o_ref[2 * pair + 1] += part[:, 128:]


def project(tok_rows, kv_weight, depth=512):
    tokens, width = tok_rows.shape
    heads, pair_width = kv_weight.shape[1:]
    return pl.pallas_call(
        project_kernel,
        grid=(width // depth,),
        out_shape=jax.ShapeDtypeStruct((heads, tokens, pair_width), F32),
        in_specs=[
            pl.BlockSpec((tokens, depth), lambda i: (0, i)),
            pl.BlockSpec((depth, heads, pair_width), lambda i: (i, 0, 0)),
        ],
        out_specs=pl.BlockSpec((heads, tokens, pair_width), lambda i: (0, 0, 0)),
        compiler_params=pltpu.CompilerParams(vmem_limit_bytes=VMEM),
        cost_estimate=small_cost(),
        name="project",
    )(tok_rows, kv_weight)


def turn_kernel(rank_ref, after_ref, x_ref, mine_ref, send_ref):
    first = rank_ref[0] == 0
    for block in range(mine_ref.shape[0]):
        even = x_ref[:, block * 256 : block * 256 + 128].T
        odd = x_ref[:, block * 256 + 128 : block * 256 + 256].T
        mine_ref[block] = jnp.where(first, even, odd)
        send_ref[block] = jnp.where(first, odd, even)


def turn(ret_rank, after, tok_rows, per_step=8):
    tokens, width = tok_rows.shape
    half = jax.ShapeDtypeStruct((N_ENC, 128, tokens), BF16)
    return pl.pallas_call(
        turn_kernel,
        grid_spec=pltpu.PrefetchScalarGridSpec(
            num_scalar_prefetch=1,
            grid=(N_ENC // per_step,),
            in_specs=[
                pl.BlockSpec(memory_space=pl.ANY),
                pl.BlockSpec((tokens, 256 * per_step), lambda i, r: (0, i)),
            ],
            out_specs=[pl.BlockSpec((per_step, 128, tokens), lambda i, r: (i, 0, 0))] * 2,
        ),
        out_shape=[half, half],
        compiler_params=pltpu.CompilerParams(vmem_limit_bytes=VMEM),
        cost_estimate=pl.CostEstimate(
            flops=0, bytes_accessed=64 << 20, transcendentals=0
        ),
        name="turn",
    )(ret_rank.reshape(1), after, tok_rows)


def local_scores(kv_ref, qd_ref, head, passage, blocks):
    pair = kv_ref[head, passage * SLOT : (passage + 1) * SLOT, :]
    high = pair.astype(BF16)
    low = (pair - high.astype(F32)).astype(BF16)
    rows = qd_ref[head, passage * LQ : (passage + 1) * LQ, :]
    lane = lax.broadcasted_iota(jnp.int32, rows.shape, 1)
    zero = jnp.zeros_like(rows)
    stacked = jnp.concatenate(
        [jnp.where(lane < HD, rows, zero), jnp.where(lane < HD, zero, rows)], axis=0
    )
    both = lax.dot_general(
        jnp.concatenate([high, low], axis=1),
        jnp.concatenate([stacked, stacked], axis=1),
        (((1,), (1,)), ((), ())),
        preferred_element_type=F32,
    )
    scores = both[:, :LQ]
    place = lax.broadcasted_iota(jnp.int32, scores.shape, 0)
    return jnp.where(place < BLK * blocks, scores, -1e30), both[:, LQ:], stacked


def stats_kernel(
    heads, question_ref, blocks_ref, kv_ref, qd_ref, score_ref, emb_ref, o_ref, late_ref, rows_ref
):
    step = pl.program_id(0)
    per_step = kv_ref.shape[0]
    for passage in range(2):
        tops, dots = [], []
        for head in range(per_step):
            scores, prob_grad, _ = local_scores(
                kv_ref, qd_ref, head, passage, blocks_ref[passage]
            )
            top = jnp.max(scores, axis=0, keepdims=True)
            expo = jnp.exp(scores - top)
            total = jnp.sum(expo, axis=0, keepdims=True)
            tops.append(top + jnp.log(total))
            dots.append(jnp.sum(expo * prob_grad, axis=0, keepdims=True) / total)
        place = passage * heads + step * per_step
        rows_ref[pl.ds(pl.multiple_of(place, 8), per_step), :] = jnp.concatenate(tops, axis=0)
        rows_ref[pl.ds(pl.multiple_of(2 * heads + place, 8), per_step), :] = jnp.concatenate(
            dots, axis=0
        )

    @pl.when(step == pl.num_programs(0) - 1)
    def _():
        rows_ref[4 * heads :, :] = score_ref[...]
        late_ref[...] = emb_ref[...]
        o_ref[...] = jnp.broadcast_to(rows_ref[...][None], o_ref.shape)


def local_stats(own_question, own_blocks, key_value, gathered, score_rows, own_emb):
    heads, tokens, pair_width = key_value.shape
    per_step = 8
    rows = 4 * heads + 8
    return pl.pallas_call(
        functools.partial(stats_kernel, heads),
        grid_spec=pltpu.PrefetchScalarGridSpec(
            num_scalar_prefetch=2,
            grid=(heads // per_step,),
            in_specs=[
                pl.BlockSpec((per_step, tokens, pair_width), lambda i, *_: (i, 0, 0)),
                pl.BlockSpec((per_step,) + gathered.shape[1:], lambda i, *_: (i, 0, 0)),
                pl.BlockSpec((8, 128), lambda i, *_: (0, 0)),
                pl.BlockSpec(own_emb.shape, lambda i, *_: (0, 0)),
            ],
            out_specs=[
                pl.BlockSpec((N_ENC, rows, 128), lambda i, *_: (0, 0, 0)),
                pl.BlockSpec(own_emb.shape, lambda i, *_: (0, 0)),
            ],
            scratch_shapes=[pltpu.VMEM((rows, 128), F32)],
        ),
        out_shape=[
            jax.ShapeDtypeStruct((N_ENC, rows, 128), F32),
            jax.ShapeDtypeStruct(own_emb.shape, F32),
        ],
        compiler_params=pltpu.CompilerParams(vmem_limit_bytes=VMEM),
        cost_estimate=small_cost(),
        name="local_stats",
    )(own_question, own_blocks, key_value, gathered, score_rows, own_emb)


def merge_stats(heads, question_ref, own_ref, order_ref, stats_ref, norm_ref, aux_ref):
    masses, shares = [], []
    for passage in range(2):
        tops, dots, marks = [], [], []
        for slot in range(PASS):
            place = order_ref[question_ref[passage] * PASS + slot]
            owner = place // 2
            at = place - 2 * owner
            tops.append(stats_ref[owner, pl.ds(pl.multiple_of(at * heads, heads), heads), :])
            dots.append(
                stats_ref[owner, pl.ds(pl.multiple_of((2 + at) * heads, heads), heads), :]
            )
            pair = stats_ref[owner, 4 * heads : 4 * heads + 8, :]
            marks.append(jnp.where(at == 0, pair[0:1], pair[1:2]))
        top = functools.reduce(jnp.maximum, tops)
        norm = top + jnp.log(sum(jnp.exp(t - top) for t in tops))
        norm_ref[passage] = norm
        norm_ref[2 + passage] = sum(jnp.exp(t - norm) * d for t, d in zip(tops, dots))
        own = stats_ref[own_ref[0], passage * heads : (passage + 1) * heads, :]
        mass = jnp.sum(jnp.exp(own - norm), axis=0, keepdims=True)
        masses.append(jnp.broadcast_to(jnp.sum(mass, axis=1, keepdims=True), (1, 128)))
        best = functools.reduce(jnp.maximum, marks)
        mark = stats_ref[own_ref[0], 4 * heads : 4 * heads + 8, :][passage : passage + 1]
        shares.append(jnp.exp(mark - best) / sum(jnp.exp(m - best) for m in marks))
    aux_ref[...] = jnp.concatenate(masses + shares + [jnp.zeros((4, 128), F32)], axis=0)


def back_heads(part, question_ref, blocks_ref, kv_ref, qd_ref, norm_ref, flat_ref):
    per_step = kv_ref.shape[0]
    first = part * 8 + pl.program_id(0) * per_step
    for passage in range(2):
        for head in range(per_step):
            scores, prob_grad, stacked = local_scores(
                kv_ref, qd_ref, head, passage, blocks_ref[passage]
            )
            norm = norm_ref[passage, pl.ds(first + head, 1), :]
            dot = norm_ref[2 + passage, pl.ds(first + head, 1), :]
            probs = jnp.exp(scores - norm)
            score_grad = probs * (prob_grad - dot)
            left = jnp.concatenate([score_grad, probs], axis=1).astype(BF16)
            grad = jnp.dot(left, stacked, preferred_element_type=F32).astype(BF16)
            flat_ref[
                passage * SLOT : (passage + 1) * SLOT, head * 128 : (head + 1) * 128
            ] = grad


def back_first_kernel(
    heads,
    question_ref,
    blocks_ref,
    own_ref,
    order_ref,
    after_ref,
    kv_ref,
    qd_ref,
    stats_ref,
    flat_ref,
    norm_ref,
    aux_ref,
):
    @pl.when(pl.program_id(0) == 0)
    def _():
        merge_stats(heads, question_ref, own_ref, order_ref, stats_ref, norm_ref, aux_ref)

    back_heads(0, question_ref, blocks_ref, kv_ref, qd_ref, norm_ref, flat_ref)


def back_second_kernel(question_ref, blocks_ref, kv_ref, qd_ref, norm_ref, flat_ref):
    back_heads(1, question_ref, blocks_ref, kv_ref, qd_ref, norm_ref, flat_ref)


BACK_COST = pl.CostEstimate(flops=0, bytes_accessed=32 << 20, transcendentals=0)


def back_specs(key_value, gathered, part, per_step):
    base = part * 8 // per_step
    tokens, pair_width = key_value.shape[1:]
    return [
        pl.BlockSpec((per_step, tokens, pair_width), lambda i, *_: (base + i, 0, 0)),
        pl.BlockSpec((per_step,) + gathered.shape[1:], lambda i, *_: (base + i, 0, 0)),
    ]


def back_first(after, own_question, own_blocks, enc_rank, order_row, key_value, gathered, stats, per_step=4):
    heads, tokens, pair_width = key_value.shape
    return pl.pallas_call(
        functools.partial(back_first_kernel, heads),
        grid_spec=pltpu.PrefetchScalarGridSpec(
            num_scalar_prefetch=4,
            grid=(8 // per_step,),
            in_specs=[pl.BlockSpec(memory_space=pl.ANY)]
            + back_specs(key_value, gathered, 0, per_step)
            + [pl.BlockSpec(stats.shape, lambda i, *_: (0, 0, 0))],
            out_specs=[
                pl.BlockSpec((tokens, per_step * pair_width), lambda i, *_: (0, i)),
                pl.BlockSpec((4, heads, 128), lambda i, *_: (0, 0, 0)),
                pl.BlockSpec((8, 128), lambda i, *_: (0, 0)),
            ],
        ),
        out_shape=[
            jax.ShapeDtypeStruct((tokens, 8 * pair_width), BF16),
            jax.ShapeDtypeStruct((4, heads, 128), F32),
            jax.ShapeDtypeStruct((8, 128), F32),
        ],
        compiler_params=pltpu.CompilerParams(vmem_limit_bytes=VMEM),
        cost_estimate=BACK_COST,
        name="back_first",
    )(own_question, own_blocks, enc_rank.reshape(1), order_row, after, key_value, gathered, stats)


def back_second(own_question, own_blocks, key_value, gathered, norms, per_step=4):
    heads, tokens, pair_width = key_value.shape
    return pl.pallas_call(
        back_second_kernel,
        grid_spec=pltpu.PrefetchScalarGridSpec(
            num_scalar_prefetch=2,
            grid=(8 // per_step,),
            in_specs=back_specs(key_value, gathered, 1, per_step)
            + [pl.BlockSpec(norms.shape, lambda i, *_: (0, 0, 0))],
            out_specs=pl.BlockSpec((tokens, per_step * pair_width), lambda i, *_: (0, i)),
        ),
        out_shape=jax.ShapeDtypeStruct((tokens, 8 * pair_width), BF16),
        compiler_params=pltpu.CompilerParams(vmem_limit_bytes=VMEM),
        cost_estimate=BACK_COST,
        name="back_second",
    )(own_question, own_blocks, key_value, gathered, norms)


def product(near_ref, far_ref, own_ref, other_ref):
    rows, depth = SIDE * 128, near_ref.shape[-1]
    total = jnp.dot(near_ref[...].reshape(rows, depth), own_ref[...], preferred_element_type=F32)
    return total + jnp.dot(
        far_ref[...].reshape(rows, depth), other_ref[...], preferred_element_type=F32
    )


def chunk_spec(part, tokens, which):
    if part == 0:
        return pl.BlockSpec((1, SIDE, 128, tokens), lambda i, w: (w[which], 0, 0, 0))
    return pl.BlockSpec((SIDE, 1, 128, tokens), lambda i, w: (0, w[which], 0, 0))


def ordered(kernel, which_ref, after_ref, *refs):
    kernel(which_ref, *refs)


def chunk_call(
    kernel, name, which, part, turned, grads, after, extra, extra_specs, out_specs, out_shape
):
    tokens, columns = grads[0].shape
    half = pl.BlockSpec((tokens, columns // 2), lambda i, w: (0, i))
    chunks = which.shape[0]
    turned_specs, turned_args = [], []
    for index in range(chunks):
        turned_specs += [chunk_spec(part, tokens, index)] * 2
        turned_args += turned
    return pl.pallas_call(
        functools.partial(ordered, kernel),
        grid_spec=pltpu.PrefetchScalarGridSpec(
            num_scalar_prefetch=1,
            grid=(2,),
            in_specs=[pl.BlockSpec(memory_space=pl.ANY)]
            + turned_specs
            + [half, half]
            + extra_specs,
            out_specs=out_specs,
        ),
        out_shape=out_shape,
        compiler_params=pltpu.CompilerParams(vmem_limit_bytes=VMEM),
        cost_estimate=small_cost(),
        name=name,
    )(which, after, *turned_args, *grads, *extra)


def far_kernel(which_ref, near_ref, far_ref, own_ref, other_ref, note_ref, a_ref, b_ref, out_ref):
    total = product(near_ref, far_ref, own_ref, other_ref).astype(BF16)

    @pl.when(pl.program_id(0) == 0)
    def _():
        a_ref[...] = total
        out_ref[...] = note_ref[...]

    @pl.when(pl.program_id(0) == 1)
    def _():
        b_ref[...] = total


def far_chunk(which, part, turned, grads, after, note):
    rows, columns = SIDE * 128, grads[0].shape[1] // 2
    half = jax.ShapeDtypeStruct((rows, columns), BF16)
    note_spec = pl.BlockSpec((8, 128), lambda i, w: (0, 0))
    half_spec = pl.BlockSpec((rows, columns), lambda i, w: (0, 0))
    return chunk_call(
        far_kernel,
        "far_chunk",
        which,
        part,
        turned,
        grads,
        after,
        [note],
        [note_spec],
        [half_spec, half_spec, note_spec],
        [half, half, jax.ShapeDtypeStruct((8, 128), F32)],
    )


def own_kernel(which_ref, near_ref, far_ref, own_ref, other_ref, o_ref):
    o_ref[0] = product(near_ref, far_ref, own_ref, other_ref).astype(BF16)


def own_chunk(which, part, turned, grads, after):
    rows, columns = SIDE * 128, grads[0].shape[1] // 2
    return chunk_call(
        own_kernel,
        "own_chunk",
        which,
        part,
        turned,
        grads,
        after,
        [],
        [],
        pl.BlockSpec((1, rows, columns), lambda i, w: (i, 0, 0)),
        jax.ShapeDtypeStruct((2, rows, columns), BF16),
    )


def side_kernel(
    which_ref, up_near, up_far, down_near, down_far, own_ref, other_ref, a_ref, b_ref, up_ref, down_ref
):
    first = pl.program_id(0) == 0
    zero = jnp.zeros(a_ref.shape, F32)
    up = product(up_near, up_far, own_ref, other_ref)
    up_ref[0] = (up + jnp.where(first, a_ref[...].astype(F32), zero)).astype(BF16)
    down = product(down_near, down_far, own_ref, other_ref)
    down_ref[0] = (down + jnp.where(first, zero, b_ref[...].astype(F32))).astype(BF16)


def side_chunks(which, part, turned, grads, after, came):
    rows, columns = SIDE * 128, grads[0].shape[1] // 2
    both = jax.ShapeDtypeStruct((2, rows, columns), BF16)
    out = pl.BlockSpec((1, rows, columns), lambda i, w: (i, 0, 0))
    full = pl.BlockSpec((rows, columns), lambda i, w: (0, 0))
    return chunk_call(
        side_kernel, "side_chunks", which, part, turned, grads, after, list(came), [full, full], [out, out], [both, both]
    )


def total_kernel(which_ref, after_ref, own_ref, up_ref, down_ref, *out_refs):
    total = own_ref[...].astype(F32) + up_ref[...].astype(F32) + down_ref[...].astype(F32)
    for step, ref in enumerate(out_refs):

        @pl.when(pl.program_id(0) == step)
        def _():
            ref[...] = total[:, 0].astype(BF16)


def totals(first, after, own, up, down):
    columns = own.shape[-1]
    cut = lambda a: a.reshape(2, SIDE, 128, columns)
    block = pl.BlockSpec((2, 1, 128, columns), lambda i, w: (0, (w[0] + i) % SIDE, 0, 0))
    out = pl.BlockSpec((2, 128, columns), lambda i, w: (0, 0, 0))
    return pl.pallas_call(
        total_kernel,
        grid_spec=pltpu.PrefetchScalarGridSpec(
            num_scalar_prefetch=1,
            grid=(SIDE,),
            in_specs=[pl.BlockSpec(memory_space=pl.ANY)] + [block] * 3,
            out_specs=[out] * SIDE,
        ),
        out_shape=[jax.ShapeDtypeStruct((2, 128, columns), BF16)] * SIDE,
        compiler_params=pltpu.CompilerParams(vmem_limit_bytes=VMEM),
        cost_estimate=small_cost(),
        name="totals",
    )(first.reshape(1), after, cut(own), cut(up), cut(down))


def gather_terms(refs):
    return sum(r[...].astype(F32) for r in refs).astype(BF16)


def first_kernel(after_ref, *refs):
    refs[-1][...] = gather_terms(refs[:-1])


def first_half(after, pieces):
    block = pl.BlockSpec(pieces[0].shape, lambda: (0, 0, 0))
    return pl.pallas_call(
        first_kernel,
        in_specs=[pl.BlockSpec(memory_space=pl.ANY)] + [block] * len(pieces),
        out_specs=block,
        out_shape=jax.ShapeDtypeStruct(pieces[0].shape, BF16),
        compiler_params=pltpu.CompilerParams(vmem_limit_bytes=16 << 20),
        cost_estimate=small_cost(),
        name="first_half",
    )(after, *pieces)


def finish_kernel(first_ref, *refs):
    heads = []
    for total in (first_ref[...], gather_terms(refs[:-1])):
        for half in range(2):
            for head in range(4):
                heads.append(total[half, :, head * 128 : (head + 1) * 128])
    refs[-1][...] = jnp.swapaxes(jnp.stack(heads), 0, 1)


def finish(first, pieces):
    return pl.pallas_call(
        finish_kernel,
        out_shape=jax.ShapeDtypeStruct((128, 16, 128), BF16),
        compiler_params=pltpu.CompilerParams(vmem_limit_bytes=VMEM),
        cost_estimate=small_cost(),
        name="finish",
    )(first, *pieces)


def by_token_kernel(after_ref, a_ref, b_ref, o_ref):
    heads = [ref[:, h * 128 : (h + 1) * 128] for ref in (a_ref, b_ref) for h in range(8)]
    o_ref[...] = jnp.swapaxes(jnp.stack(heads), 0, 1)


def by_token(after, a, b, rows=128):
    tokens, columns = a.shape
    block = pl.BlockSpec((rows, columns), lambda i: (i, 0))
    return pl.pallas_call(
        by_token_kernel,
        grid=(tokens // rows,),
        in_specs=[pl.BlockSpec(memory_space=pl.ANY), block, block],
        out_specs=pl.BlockSpec((rows, 16, 128), lambda i: (i, 0, 0)),
        out_shape=jax.ShapeDtypeStruct((tokens, 16, 128), BF16),
        compiler_params=pltpu.CompilerParams(vmem_limit_bytes=VMEM),
        cost_estimate=small_cost(),
        name="by_token",
    )(after, a, b)


def add_kernel(after_ref, a_ref, b_ref, o_ref):
    o_ref[...] = (a_ref[...].astype(F32) + b_ref[...].astype(F32)).astype(BF16)


def add_after(after, a, b):
    block = pl.BlockSpec(a.shape, lambda: (0, 0))
    return pl.pallas_call(
        add_kernel,
        in_specs=[pl.BlockSpec(memory_space=pl.ANY), block, block],
        out_specs=block,
        out_shape=jax.ShapeDtypeStruct(a.shape, BF16),
        compiler_params=pltpu.CompilerParams(vmem_limit_bytes=8 << 20),
        cost_estimate=small_cost(),
        name="add_after",
    )(after, a, b)


def gap_kernel(heads_rows, rank_ref, aux_ref, m1_ref, m2_ref, m3_ref, part_ref, gate_ref, keep_ref, give_ref):
    rows = keep_ref.shape[0]
    mass = (aux_ref[0:2] + m1_ref[0:2]) + (m2_ref[0:2] + m3_ref[0:2])
    gap = aux_ref[2:4] - mass / heads_rows
    rank = rank_ref[0]

    def at(place):
        here = pl.ds(pl.multiple_of(place * rows, 8), rows)
        return gap[0:1, 0:1] * part_ref[0, here, :] + gap[1:2, 0:1] * part_ref[1, here, :]

    keep_ref[...] = at(rank)
    give_ref[...] = at(1 - rank).astype(BF16)


def apply_gap(ret_rank, aux, masses, parts, heads_rows, gate):
    _, rows, columns = parts.shape
    whole = lambda *shape: pl.BlockSpec(shape, lambda i, r: (0,) * len(shape))
    return pl.pallas_call(
        functools.partial(gap_kernel, float(heads_rows)),
        grid_spec=pltpu.PrefetchScalarGridSpec(
            num_scalar_prefetch=1,
            grid=(1,),
            in_specs=[whole(8, 128)] * 4
            + [whole(2, rows, columns), pl.BlockSpec(memory_space=pl.ANY)],
            out_specs=[whole(rows // 2, columns)] * 2,
        ),
        out_shape=[
            jax.ShapeDtypeStruct((rows // 2, columns), F32),
            jax.ShapeDtypeStruct((rows // 2, columns), BF16),
        ],
        compiler_params=pltpu.CompilerParams(vmem_limit_bytes=VMEM),
        cost_estimate=small_cost(),
        name="apply_gap",
    )(ret_rank.reshape(1), aux, *masses, parts, gate)


def ring_pairs(axis, step):
    pairs = []
    for x in range(SIDE):
        for y in range(SIDE):
            to = ((x + step) % SIDE, y) if axis == 0 else (x, (y + step) % SIDE)
            pairs.append((x * SIDE + y, to[0] * SIDE + to[1]))
    return pairs


def send(value, axis, step):
    return lax.ppermute(value, "enc", ring_pairs(axis, step))


def add(*terms):
    return sum(t.astype(F32) for t in terms).astype(BF16)


def on_device(
    enc_states,
    kv_weight,
    queries,
    out_grad,
    passage_order,
    passage_blocks,
    ret_tokens,
    ret_weight,
    question_emb,
):
    pass_dev, _, slot_len, width = enc_states.shape
    heads, pair_width = kv_weight.shape[1:]
    question_count, query_len = queries.shape[:2]
    enc_rank = lax.axis_index("enc")
    dec_rank = lax.axis_index("dec")
    ret_rank = lax.axis_index("ret")
    order_row = passage_order[0]
    blocks_row = passage_blocks[0]
    tokens = pass_dev * slot_len
    swap = [(0, 1), (1, 0)]

    rows = question_count * query_len
    packed = pack(order_row, queries.reshape(rows, HD), out_grad.reshape(rows, HD))
    gathered = lax.all_to_all(
        packed.reshape(N_ENC, pass_dev * query_len, pair_width),
        "enc",
        split_axis=0,
        concat_axis=0,
        tiled=True,
    )

    tok_rows = enc_states.reshape(tokens, width)
    key_value = project(tok_rows, kv_weight)

    own_pass = enc_rank * pass_dev + jnp.arange(pass_dev, dtype=jnp.int32)
    slot_of = jnp.sum(
        jnp.where(
            order_row[None, :] == own_pass[:, None],
            jnp.arange(order_row.shape[0], dtype=jnp.int32)[None, :],
            0,
        ),
        axis=1,
    )
    own_question = slot_of // PASS
    own_blocks = lax.dynamic_slice_in_dim(blocks_row, enc_rank * pass_dev, pass_dev)
    own_emb = jnp.sum(
        jnp.where(
            (own_question[:, None] == jnp.arange(question_count)[None, :])[..., None],
            question_emb[None],
            0.0,
        ),
        axis=1,
    )
    ret_rows = ret_tokens.reshape(tokens, ret_tokens.shape[3])
    ret_width = ret_rows.shape[1]
    pre_act = jnp.dot(ret_rows, ret_weight, preferred_element_type=F32).reshape(
        pass_dev, slot_len, ret_width
    )
    own_live = jnp.arange(slot_len, dtype=jnp.int32)[None, :] < BLK * own_blocks[:, None]
    own_length = (BLK * own_blocks).astype(F32)
    embed_own = (
        jnp.sum(jnp.where(own_live[..., None], jax.nn.gelu(pre_act), 0.0), axis=1)
        / own_length[:, None]
    )
    own_score = jnp.sum(own_emb * embed_own, axis=-1)
    score_rows = jnp.broadcast_to(
        jnp.concatenate([own_score, jnp.zeros((8 - pass_dev,), F32)])[:, None], (8, 128)
    )

    stats, late_emb = local_stats(
        own_question, own_blocks, key_value, gathered, score_rows, own_emb
    )
    mine, to_send = turn(ret_rank, stats, tok_rows)
    other = lax.ppermute(to_send, "ret", swap)
    hidden_grad = jnp.where(
        own_live[..., None], (late_emb / own_length[:, None])[:, None, :], 0.0
    )
    pre_grad = gelu_grad(pre_act, hidden_grad).astype(BF16)
    share = ret_width // N_DEC
    part_rows = lax.dynamic_slice_in_dim(ret_rows, dec_rank * share, share, axis=1)
    ret_parts = lax.dot_general(
        part_rows.reshape(pass_dev, slot_len, share),
        pre_grad,
        (((1,), (1,)), ((0,), (0,))),
        preferred_element_type=F32,
    )
    stats_all = lax.all_to_all(stats, "enc", split_axis=0, concat_axis=0, tiled=True)
    flat_a, norms, aux = back_first(
        ret_parts, own_question, own_blocks, enc_rank, order_row, key_value, gathered, stats_all
    )
    far_a = lax.ppermute(flat_a, "ret", swap)
    flat_b = back_second(own_question, own_blocks, key_value, gathered, norms)
    far_b = lax.ppermute(flat_b, "ret", swap)

    turned = [
        mine.reshape(SIDE, SIDE, 128, tokens),
        other.reshape(SIDE, SIDE, 128, tokens),
    ]
    grads = [[flat_a, far_a], [flat_b, far_b]]
    at = (enc_rank // SIDE, enc_rank % SIDE)
    steps = lambda part, *ks: (at[part] + jnp.array(ks, jnp.int32)) % SIDE
    def level(after, half, bit):
        far = lax.ppermute(half, "enc", [(i, i ^ bit) for i in range(N_ENC)])
        return add_after(after, half, far)

    a, b, aux = far_chunk(steps(0, 2), 0, turned, grads[0], norms, aux)
    came = [(send(a, 0, 1), send(b, 0, -1))]
    masses = [
        lax.ppermute(aux, "dec", [(i, (i + step) % N_DEC) for i in range(N_DEC)])
        for step in range(1, N_DEC)
    ]
    a, b, late_aux = far_chunk(steps(1, 2), 1, turned, grads[1], a, aux)
    came.append((send(a, 1, 1), send(b, 1, -1)))
    keep, give = apply_gap(
        ret_rank, late_aux, masses, ret_parts, N_DEC * heads * query_len, a
    )
    own = [own_chunk(steps(0, 0), 0, turned, grads[0], give)]
    half = add_after(own[0], keep, lax.ppermute(give, "ret", swap))
    up, down = side_chunks(steps(0, 1, 3), 0, turned, grads[0], half, came[0])
    sent = [(send(up, 0, 1), send(down, 0, -1))]
    half = level(up, half, 4)
    up, down = side_chunks(steps(1, 1, 3), 1, turned, grads[1], half, came[1])
    sent.append((send(up, 1, 1), send(down, 1, -1)))
    half = level(up, half, 1)
    own.append(own_chunk(steps(1, 0), 1, turned, grads[1], half))
    half = level(own[1], half, 8)
    by_tokens = by_token(half, flat_a, flat_b)
    kv_grad = by_tokens.reshape(pass_dev, 1, slot_len, heads, pair_width)
    half = level(by_tokens, half, 2)
    pieces, last = [], half
    for part in range(2):
        cuts = totals(at[1 - part], last, own[part], *sent[part])
        pieces.append([cuts[0]] + [send(cuts[k], 1 - part, k) for k in range(1, SIDE)])
        last = cuts[0]
    summed = first_half(cuts[0], pieces[0])
    weight_total = finish(summed, pieces[1])

    half_far = lax.ppermute(half, "ret", swap)
    quarter = jnp.where(
        ret_rank == 0, jnp.stack([half, half_far]), jnp.stack([half_far, half])
    ).reshape(share, ret_width)
    ret_weight_grad = jnp.zeros((N_DEC, share, ret_width), BF16)
    for step in range(N_DEC):
        piece = quarter
        if step:
            piece = lax.ppermute(
                quarter, "dec", [(i, (i + step) % N_DEC) for i in range(N_DEC)]
            )
        ret_weight_grad = lax.dynamic_update_index_in_dim(
            ret_weight_grad, piece, (dec_rank - step) % N_DEC, 0
        )
    return (kv_grad, weight_total, ret_weight_grad.reshape(ret_width, ret_width))


def solution(mesh):
    return jax.shard_map(
        on_device,
        mesh=mesh,
        in_specs=(
            P("enc", "ret", None, None),
            P(None, "dec", None),
            P("ret", None, ("dec", "enc"), None),
            P("ret", None, ("dec", "enc"), None),
            P("ret", None),
            P("ret", None),
            P("enc", "ret", None, None),
            P(),
            P("ret", None),
        ),
        out_specs=(P("enc", "ret", None, "dec", None), P(("enc", "ret"), "dec", None), P()),
        check_vma=False,
    )
```

```python
import functools

import jax
import jax.numpy as jnp
from jax import lax
from jax.experimental import pallas as pl
from jax.experimental.pallas import tpu as pltpu
from jax.sharding import PartitionSpec as P

BLK = 128
PASS = 8
N_ENC = 16
SIDE = 4
N_DEC = 4
LQ = 128
HD = 64
SLOT = 256
F32 = jnp.float32
BF16 = jnp.bfloat16
VMEM = 60 << 20


def small_cost():
    return pl.CostEstimate(flops=1 << 10, bytes_accessed=1 << 10, transcendentals=0)


def gelu_grad(pre_act, upstream):
    return jax.vjp(jax.nn.gelu, pre_act)[1](upstream)[0]


def pack_kernel(order_ref, q_ref, d_ref, o_ref):
    rows = o_ref.shape[1]
    packed = []
    for question in range(q_ref.shape[0] // rows):
        at = slice(question * rows, (question + 1) * rows)
        packed.append(
            jnp.concatenate([q_ref[at] * jnp.asarray(0.125, BF16), d_ref[at]], axis=1)
        )
    for slot in range(o_ref.shape[0]):
        o_ref[order_ref[slot]] = packed[slot // PASS]


def pack(order_row, q_rows, d_rows):
    total, head_dim = q_rows.shape
    passages = order_row.shape[0]
    return pl.pallas_call(
        pack_kernel,
        grid_spec=pltpu.PrefetchScalarGridSpec(
            num_scalar_prefetch=1,
            grid=(1,),
            in_specs=[pl.BlockSpec((total, head_dim), lambda i, o: (0, 0))] * 2,
            out_specs=pl.BlockSpec((passages, LQ, 2 * head_dim), lambda i, o: (0, 0, 0)),
        ),
        out_shape=jax.ShapeDtypeStruct((passages, LQ, 2 * head_dim), BF16),
        compiler_params=pltpu.CompilerParams(vmem_limit_bytes=VMEM),
        cost_estimate=small_cost(),
        name="pack",
    )(order_row, q_rows, d_rows)


def project_kernel(x_ref, w_ref, o_ref):
    @pl.when(pl.program_id(0) == 0)
    def _():
        o_ref[...] = jnp.zeros_like(o_ref)

    rows = x_ref[...]
    by_head = jnp.swapaxes(w_ref[...], 0, 1)
    for pair in range(by_head.shape[0] // 2):
        both = jnp.concatenate([by_head[2 * pair], by_head[2 * pair + 1]], axis=1)
        part = jnp.dot(rows, both, preferred_element_type=F32)
        o_ref[2 * pair] += part[:, :128]
        o_ref[2 * pair + 1] += part[:, 128:]


def project(tok_rows, kv_weight, depth=512):
    tokens, width = tok_rows.shape
    heads, pair_width = kv_weight.shape[1:]
    return pl.pallas_call(
        project_kernel,
        grid=(width // depth,),
        out_shape=jax.ShapeDtypeStruct((heads, tokens, pair_width), F32),
        in_specs=[
            pl.BlockSpec((tokens, depth), lambda i: (0, i)),
            pl.BlockSpec((depth, heads, pair_width), lambda i: (i, 0, 0)),
        ],
        out_specs=pl.BlockSpec((heads, tokens, pair_width), lambda i: (0, 0, 0)),
        compiler_params=pltpu.CompilerParams(vmem_limit_bytes=VMEM),
        cost_estimate=small_cost(),
        name="project",
    )(tok_rows, kv_weight)


def turn_kernel(rank_ref, after_ref, x_ref, mine_ref, send_ref):
    first = rank_ref[0] == 0
    for block in range(mine_ref.shape[0]):
        even = x_ref[:, block * 256 : block * 256 + 128].T
        odd = x_ref[:, block * 256 + 128 : block * 256 + 256].T
        mine_ref[block] = jnp.where(first, even, odd)
        send_ref[block] = jnp.where(first, odd, even)


def turn(ret_rank, after, tok_rows, per_step=8):
    tokens, width = tok_rows.shape
    half = jax.ShapeDtypeStruct((N_ENC, 128, tokens), BF16)
    return pl.pallas_call(
        turn_kernel,
        grid_spec=pltpu.PrefetchScalarGridSpec(
            num_scalar_prefetch=1,
            grid=(N_ENC // per_step,),
            in_specs=[
                pl.BlockSpec(memory_space=pl.ANY),
                pl.BlockSpec((tokens, 256 * per_step), lambda i, r: (0, i)),
            ],
            out_specs=[pl.BlockSpec((per_step, 128, tokens), lambda i, r: (i, 0, 0))] * 2,
        ),
        out_shape=[half, half],
        compiler_params=pltpu.CompilerParams(vmem_limit_bytes=VMEM),
        cost_estimate=pl.CostEstimate(
            flops=0, bytes_accessed=64 << 20, transcendentals=0
        ),
        name="turn",
    )(ret_rank.reshape(1), after, tok_rows)


def local_scores(kv_ref, qd_ref, head, passage, blocks):
    pair = kv_ref[head, passage * SLOT : (passage + 1) * SLOT, :]
    high = pair.astype(BF16)
    low = (pair - high.astype(F32)).astype(BF16)
    rows = qd_ref[head, passage * LQ : (passage + 1) * LQ, :]
    lane = lax.broadcasted_iota(jnp.int32, rows.shape, 1)
    zero = jnp.zeros_like(rows)
    stacked = jnp.concatenate(
        [jnp.where(lane < HD, rows, zero), jnp.where(lane < HD, zero, rows)], axis=0
    )
    both = lax.dot_general(
        jnp.concatenate([high, low], axis=1),
        jnp.concatenate([stacked, stacked], axis=1),
        (((1,), (1,)), ((), ())),
        preferred_element_type=F32,
    )
    scores = both[:, :LQ]
    place = lax.broadcasted_iota(jnp.int32, scores.shape, 0)
    return jnp.where(place < BLK * blocks, scores, -1e30), both[:, LQ:], stacked


def stats_kernel(
    heads, question_ref, blocks_ref, kv_ref, qd_ref, score_ref, emb_ref, o_ref, late_ref, rows_ref
):
    step = pl.program_id(0)
    per_step = kv_ref.shape[0]
    for passage in range(2):
        tops, dots = [], []
        for head in range(per_step):
            scores, prob_grad, _ = local_scores(
                kv_ref, qd_ref, head, passage, blocks_ref[passage]
            )
            top = jnp.max(scores, axis=0, keepdims=True)
            expo = jnp.exp(scores - top)
            total = jnp.sum(expo, axis=0, keepdims=True)
            tops.append(top + jnp.log(total))
            dots.append(jnp.sum(expo * prob_grad, axis=0, keepdims=True) / total)
        place = passage * heads + step * per_step
        rows_ref[pl.ds(pl.multiple_of(place, 8), per_step), :] = jnp.concatenate(tops, axis=0)
        rows_ref[pl.ds(pl.multiple_of(2 * heads + place, 8), per_step), :] = jnp.concatenate(
            dots, axis=0
        )

    @pl.when(step == pl.num_programs(0) - 1)
    def _():
        rows_ref[4 * heads :, :] = score_ref[...]
        late_ref[...] = emb_ref[...]
        o_ref[...] = jnp.broadcast_to(rows_ref[...][None], o_ref.shape)


def local_stats(own_question, own_blocks, key_value, gathered, score_rows, own_emb):
    heads, tokens, pair_width = key_value.shape
    per_step = 8
    rows = 4 * heads + 8
    return pl.pallas_call(
        functools.partial(stats_kernel, heads),
        grid_spec=pltpu.PrefetchScalarGridSpec(
            num_scalar_prefetch=2,
            grid=(heads // per_step,),
            in_specs=[
                pl.BlockSpec((per_step, tokens, pair_width), lambda i, *_: (i, 0, 0)),
                pl.BlockSpec((per_step,) + gathered.shape[1:], lambda i, *_: (i, 0, 0)),
                pl.BlockSpec((8, 128), lambda i, *_: (0, 0)),
                pl.BlockSpec(own_emb.shape, lambda i, *_: (0, 0)),
            ],
            out_specs=[
                pl.BlockSpec((N_ENC, rows, 128), lambda i, *_: (0, 0, 0)),
                pl.BlockSpec(own_emb.shape, lambda i, *_: (0, 0)),
            ],
            scratch_shapes=[pltpu.VMEM((rows, 128), F32)],
        ),
        out_shape=[
            jax.ShapeDtypeStruct((N_ENC, rows, 128), F32),
            jax.ShapeDtypeStruct(own_emb.shape, F32),
        ],
        compiler_params=pltpu.CompilerParams(vmem_limit_bytes=VMEM),
        cost_estimate=small_cost(),
        name="local_stats",
    )(own_question, own_blocks, key_value, gathered, score_rows, own_emb)


def merge_stats(heads, question_ref, own_ref, order_ref, stats_ref, norm_ref, aux_ref):
    masses, shares = [], []
    for passage in range(2):
        tops, dots, marks = [], [], []
        for slot in range(PASS):
            place = order_ref[question_ref[passage] * PASS + slot]
            owner = place // 2
            at = place - 2 * owner
            tops.append(stats_ref[owner, pl.ds(pl.multiple_of(at * heads, heads), heads), :])
            dots.append(
                stats_ref[owner, pl.ds(pl.multiple_of((2 + at) * heads, heads), heads), :]
            )
            pair = stats_ref[owner, 4 * heads : 4 * heads + 8, :]
            marks.append(jnp.where(at == 0, pair[0:1], pair[1:2]))
        top = functools.reduce(jnp.maximum, tops)
        norm = top + jnp.log(sum(jnp.exp(t - top) for t in tops))
        norm_ref[passage] = norm
        norm_ref[2 + passage] = sum(jnp.exp(t - norm) * d for t, d in zip(tops, dots))
        own = stats_ref[own_ref[0], passage * heads : (passage + 1) * heads, :]
        mass = jnp.sum(jnp.exp(own - norm), axis=0, keepdims=True)
        masses.append(jnp.broadcast_to(jnp.sum(mass, axis=1, keepdims=True), (1, 128)))
        best = functools.reduce(jnp.maximum, marks)
        mark = stats_ref[own_ref[0], 4 * heads : 4 * heads + 8, :][passage : passage + 1]
        shares.append(jnp.exp(mark - best) / sum(jnp.exp(m - best) for m in marks))
    aux_ref[...] = jnp.concatenate(masses + shares + [jnp.zeros((4, 128), F32)], axis=0)


def back_heads(part, question_ref, blocks_ref, kv_ref, qd_ref, norm_ref, flat_ref):
    per_step = kv_ref.shape[0]
    first = part * 8 + pl.program_id(0) * per_step
    for passage in range(2):
        for head in range(per_step):
            scores, prob_grad, stacked = local_scores(
                kv_ref, qd_ref, head, passage, blocks_ref[passage]
            )
            norm = norm_ref[passage, pl.ds(first + head, 1), :]
            dot = norm_ref[2 + passage, pl.ds(first + head, 1), :]
            probs = jnp.exp(scores - norm)
            score_grad = probs * (prob_grad - dot)
            left = jnp.concatenate([score_grad, probs], axis=1).astype(BF16)
            grad = jnp.dot(left, stacked, preferred_element_type=F32).astype(BF16)
            flat_ref[
                passage * SLOT : (passage + 1) * SLOT, head * 128 : (head + 1) * 128
            ] = grad


def back_first_kernel(
    heads,
    question_ref,
    blocks_ref,
    own_ref,
    order_ref,
    after_ref,
    also_ref,
    kv_ref,
    qd_ref,
    stats_ref,
    flat_ref,
    norm_ref,
    aux_ref,
):
    @pl.when(pl.program_id(0) == 0)
    def _():
        merge_stats(heads, question_ref, own_ref, order_ref, stats_ref, norm_ref, aux_ref)

    back_heads(0, question_ref, blocks_ref, kv_ref, qd_ref, norm_ref, flat_ref)


def back_second_kernel(question_ref, blocks_ref, kv_ref, qd_ref, norm_ref, flat_ref):
    back_heads(1, question_ref, blocks_ref, kv_ref, qd_ref, norm_ref, flat_ref)


BACK_COST = pl.CostEstimate(flops=0, bytes_accessed=32 << 20, transcendentals=0)


def back_specs(key_value, gathered, part, per_step):
    base = part * 8 // per_step
    tokens, pair_width = key_value.shape[1:]
    return [
        pl.BlockSpec((per_step, tokens, pair_width), lambda i, *_: (base + i, 0, 0)),
        pl.BlockSpec((per_step,) + gathered.shape[1:], lambda i, *_: (base + i, 0, 0)),
    ]


def back_first(after, own_question, own_blocks, enc_rank, order_row, key_value, gathered, stats, per_step=4):
    heads, tokens, pair_width = key_value.shape
    return pl.pallas_call(
        functools.partial(back_first_kernel, heads),
        grid_spec=pltpu.PrefetchScalarGridSpec(
            num_scalar_prefetch=4,
            grid=(8 // per_step,),
            in_specs=[pl.BlockSpec(memory_space=pl.ANY)] * 2
            + back_specs(key_value, gathered, 0, per_step)
            + [pl.BlockSpec(stats.shape, lambda i, *_: (0, 0, 0))],
            out_specs=[
                pl.BlockSpec((tokens, per_step * pair_width), lambda i, *_: (0, i)),
                pl.BlockSpec((4, heads, 128), lambda i, *_: (0, 0, 0)),
                pl.BlockSpec((8, 128), lambda i, *_: (0, 0)),
            ],
        ),
        out_shape=[
            jax.ShapeDtypeStruct((tokens, 8 * pair_width), BF16),
            jax.ShapeDtypeStruct((4, heads, 128), F32),
            jax.ShapeDtypeStruct((8, 128), F32),
        ],
        compiler_params=pltpu.CompilerParams(vmem_limit_bytes=VMEM),
        cost_estimate=BACK_COST,
        name="back_first",
    )(own_question, own_blocks, enc_rank.reshape(1), order_row, *after, key_value, gathered, stats)


def back_second(own_question, own_blocks, key_value, gathered, norms, per_step=4):
    heads, tokens, pair_width = key_value.shape
    return pl.pallas_call(
        back_second_kernel,
        grid_spec=pltpu.PrefetchScalarGridSpec(
            num_scalar_prefetch=2,
            grid=(8 // per_step,),
            in_specs=back_specs(key_value, gathered, 1, per_step)
            + [pl.BlockSpec(norms.shape, lambda i, *_: (0, 0, 0))],
            out_specs=pl.BlockSpec((tokens, per_step * pair_width), lambda i, *_: (0, i)),
        ),
        out_shape=jax.ShapeDtypeStruct((tokens, 8 * pair_width), BF16),
        compiler_params=pltpu.CompilerParams(vmem_limit_bytes=VMEM),
        cost_estimate=BACK_COST,
        name="back_second",
    )(own_question, own_blocks, key_value, gathered, norms)


def product(near_ref, far_ref, own_ref, other_ref):
    rows, depth = SIDE * 128, near_ref.shape[-1]
    total = jnp.dot(near_ref[...].reshape(rows, depth), own_ref[...], preferred_element_type=F32)
    return total + jnp.dot(
        far_ref[...].reshape(rows, depth), other_ref[...], preferred_element_type=F32
    )


def chunk_spec(part, tokens, which):
    if part == 0:
        return pl.BlockSpec((1, SIDE, 128, tokens), lambda i, w: (w[which], 0, 0, 0))
    return pl.BlockSpec((SIDE, 1, 128, tokens), lambda i, w: (0, w[which], 0, 0))


def ordered(kernel, which_ref, after_ref, also_ref, *refs):
    kernel(which_ref, *refs)


def chunk_call(
    kernel, name, which, part, turned, grads, after, extra, extra_specs, out_specs, out_shape
):
    after = after if isinstance(after, tuple) else (after, after)
    tokens, columns = grads[0].shape
    half = pl.BlockSpec((tokens, columns // 2), lambda i, w: (0, i))
    chunks = which.shape[0]
    turned_specs, turned_args = [], []
    for index in range(chunks):
        turned_specs += [chunk_spec(part, tokens, index)] * 2
        turned_args += turned
    return pl.pallas_call(
        functools.partial(ordered, kernel),
        grid_spec=pltpu.PrefetchScalarGridSpec(
            num_scalar_prefetch=1,
            grid=(2,),
            in_specs=[pl.BlockSpec(memory_space=pl.ANY)] * 2
            + turned_specs
            + [half, half]
            + extra_specs,
            out_specs=out_specs,
        ),
        out_shape=out_shape,
        compiler_params=pltpu.CompilerParams(vmem_limit_bytes=VMEM),
        cost_estimate=small_cost(),
        name=name,
    )(which, *after, *turned_args, *grads, *extra)


def far_kernel(which_ref, near_ref, far_ref, own_ref, other_ref, a_ref, b_ref):
    total = product(near_ref, far_ref, own_ref, other_ref).astype(BF16)

    @pl.when(pl.program_id(0) == 0)
    def _():
        a_ref[...] = total

    @pl.when(pl.program_id(0) == 1)
    def _():
        b_ref[...] = total


def far_chunk(which, part, turned, grads, after):
    rows, columns = SIDE * 128, grads[0].shape[1] // 2
    half = jax.ShapeDtypeStruct((rows, columns), BF16)
    half_spec = pl.BlockSpec((rows, columns), lambda i, w: (0, 0))
    return chunk_call(
        far_kernel, "far_chunk", which, part, turned, grads, after, [], [], [half_spec] * 2, [half] * 2
    )


def own_kernel(which_ref, near_ref, far_ref, own_ref, other_ref, o_ref):
    o_ref[0] = product(near_ref, far_ref, own_ref, other_ref).astype(BF16)


def own_chunk(which, part, turned, grads, after):
    rows, columns = SIDE * 128, grads[0].shape[1] // 2
    return chunk_call(
        own_kernel,
        "own_chunk",
        which,
        part,
        turned,
        grads,
        after,
        [],
        [],
        pl.BlockSpec((1, rows, columns), lambda i, w: (i, 0, 0)),
        jax.ShapeDtypeStruct((2, rows, columns), BF16),
    )


def side_kernel(
    which_ref, up_near, up_far, down_near, down_far, own_ref, other_ref, a_ref, b_ref, up_ref, down_ref
):
    first = pl.program_id(0) == 0
    zero = jnp.zeros(a_ref.shape, F32)
    up = product(up_near, up_far, own_ref, other_ref)
    up_ref[0] = (up + jnp.where(first, a_ref[...].astype(F32), zero)).astype(BF16)
    down = product(down_near, down_far, own_ref, other_ref)
    down_ref[0] = (down + jnp.where(first, zero, b_ref[...].astype(F32))).astype(BF16)


def side_chunks(which, part, turned, grads, after, came):
    rows, columns = SIDE * 128, grads[0].shape[1] // 2
    both = jax.ShapeDtypeStruct((2, rows, columns), BF16)
    out = pl.BlockSpec((1, rows, columns), lambda i, w: (i, 0, 0))
    full = pl.BlockSpec((rows, columns), lambda i, w: (0, 0))
    return chunk_call(
        side_kernel, "side_chunks", which, part, turned, grads, after, list(came), [full, full], [out, out], [both, both]
    )


def total_kernel(which_ref, after_ref, also_ref, own_ref, up_ref, down_ref, *out_refs):
    total = own_ref[...].astype(F32) + up_ref[...].astype(F32) + down_ref[...].astype(F32)
    for step, ref in enumerate(out_refs):

        @pl.when(pl.program_id(0) == step)
        def _():
            ref[...] = total[:, 0].astype(BF16)


def totals(first, after, own, up, down):
    columns = own.shape[-1]
    cut = lambda a: a.reshape(2, SIDE, 128, columns)
    block = pl.BlockSpec((2, 1, 128, columns), lambda i, w: (0, (w[0] + i) % SIDE, 0, 0))
    out = pl.BlockSpec((2, 128, columns), lambda i, w: (0, 0, 0))
    return pl.pallas_call(
        total_kernel,
        grid_spec=pltpu.PrefetchScalarGridSpec(
            num_scalar_prefetch=1,
            grid=(SIDE,),
            in_specs=[pl.BlockSpec(memory_space=pl.ANY)] * 2 + [block] * 3,
            out_specs=[out] * SIDE,
        ),
        out_shape=[jax.ShapeDtypeStruct((2, 128, columns), BF16)] * SIDE,
        compiler_params=pltpu.CompilerParams(vmem_limit_bytes=VMEM),
        cost_estimate=small_cost(),
        name="totals",
    )(first.reshape(1), *after, cut(own), cut(up), cut(down))


def gather_terms(refs):
    return sum(r[...].astype(F32) for r in refs).astype(BF16)


def first_kernel(after_ref, *refs):
    refs[-1][...] = gather_terms(refs[:-1])


def first_half(after, pieces):
    block = pl.BlockSpec(pieces[0].shape, lambda: (0, 0, 0))
    return pl.pallas_call(
        first_kernel,
        in_specs=[pl.BlockSpec(memory_space=pl.ANY)] + [block] * len(pieces),
        out_specs=block,
        out_shape=jax.ShapeDtypeStruct(pieces[0].shape, BF16),
        compiler_params=pltpu.CompilerParams(vmem_limit_bytes=VMEM),
        cost_estimate=small_cost(),
        name="first_half",
    )(after, *pieces)


def finish_kernel(first_ref, *refs):
    heads = []
    for total in (first_ref[...], gather_terms(refs[:-1])):
        for half in range(2):
            for head in range(4):
                heads.append(total[half, :, head * 128 : (head + 1) * 128])
    refs[-1][...] = jnp.swapaxes(jnp.stack(heads), 0, 1)


def finish(first, pieces):
    return pl.pallas_call(
        finish_kernel,
        out_shape=jax.ShapeDtypeStruct((128, 16, 128), BF16),
        compiler_params=pltpu.CompilerParams(vmem_limit_bytes=VMEM),
        cost_estimate=small_cost(),
        name="finish",
    )(first, *pieces)


def by_token_kernel(after_ref, a_ref, b_ref, o_ref):
    heads = [ref[:, h * 128 : (h + 1) * 128] for ref in (a_ref, b_ref) for h in range(8)]
    o_ref[...] = jnp.swapaxes(jnp.stack(heads), 0, 1)


def by_token(after, a, b, rows=128):
    tokens, columns = a.shape
    block = pl.BlockSpec((rows, columns), lambda i: (i, 0))
    return pl.pallas_call(
        by_token_kernel,
        grid=(tokens // rows,),
        in_specs=[pl.BlockSpec(memory_space=pl.ANY), block, block],
        out_specs=pl.BlockSpec((rows, 16, 128), lambda i: (i, 0, 0)),
        out_shape=jax.ShapeDtypeStruct((tokens, 16, 128), BF16),
        compiler_params=pltpu.CompilerParams(vmem_limit_bytes=VMEM),
        cost_estimate=small_cost(),
        name="by_token",
    )(after, a, b)


def add_after(after, a, b):
    a, after = lax.optimization_barrier((a, after))
    return add(a, b)


def gap_kernel(heads_rows, rank_ref, aux_ref, m1_ref, m2_ref, m3_ref, part_ref, gate_ref, keep_ref, give_ref):
    rows = keep_ref.shape[0]
    mass = (aux_ref[0:2] + m1_ref[0:2]) + (m2_ref[0:2] + m3_ref[0:2])
    gap = aux_ref[2:4] - mass / heads_rows
    rank = rank_ref[0]

    def at(place):
        here = pl.ds(pl.multiple_of(place * rows, 8), rows)
        return gap[0:1, 0:1] * part_ref[0, here, :] + gap[1:2, 0:1] * part_ref[1, here, :]

    keep_ref[...] = at(rank)
    give_ref[...] = at(1 - rank).astype(BF16)


def apply_gap(ret_rank, aux, masses, parts, heads_rows, gate):
    _, rows, columns = parts.shape
    whole = lambda *shape: pl.BlockSpec(shape, lambda i, r: (0,) * len(shape))
    return pl.pallas_call(
        functools.partial(gap_kernel, float(heads_rows)),
        grid_spec=pltpu.PrefetchScalarGridSpec(
            num_scalar_prefetch=1,
            grid=(1,),
            in_specs=[whole(8, 128)] * 4
            + [whole(2, rows, columns), pl.BlockSpec(memory_space=pl.ANY)],
            out_specs=[whole(rows // 2, columns)] * 2,
        ),
        out_shape=[
            jax.ShapeDtypeStruct((rows // 2, columns), F32),
            jax.ShapeDtypeStruct((rows // 2, columns), BF16),
        ],
        compiler_params=pltpu.CompilerParams(vmem_limit_bytes=VMEM),
        cost_estimate=small_cost(),
        name="apply_gap",
    )(ret_rank.reshape(1), aux, *masses, parts, gate)


def ring_pairs(axis, step):
    pairs = []
    for x in range(SIDE):
        for y in range(SIDE):
            to = ((x + step) % SIDE, y) if axis == 0 else (x, (y + step) % SIDE)
            pairs.append((x * SIDE + y, to[0] * SIDE + to[1]))
    return pairs


def send(value, axis, step):
    return lax.ppermute(value, "enc", ring_pairs(axis, step))


def add(*terms):
    return sum(t.astype(F32) for t in terms).astype(BF16)


def join_kernel(low_ref, after_ref, own_ref, far_ref, o_ref):
    rows = own_ref.shape[0]
    low = low_ref[0] == 1
    own, far = own_ref[...], far_ref[...]
    o_ref[:rows] = jnp.where(low, own, far)
    o_ref[rows:] = jnp.where(low, far, own)


def joined(after, block, far, bit, rank):
    rows, columns = block.shape
    low = ((rank & bit) == 0).astype(jnp.int32).reshape(1)
    half = pl.BlockSpec((rows, columns), lambda i, r: (0, 0))
    return pl.pallas_call(
        join_kernel,
        grid_spec=pltpu.PrefetchScalarGridSpec(
            num_scalar_prefetch=1,
            grid=(1,),
            in_specs=[pl.BlockSpec(memory_space=pl.ANY), half, half],
            out_specs=pl.BlockSpec((2 * rows, columns), lambda i, r: (0, 0)),
        ),
        out_shape=jax.ShapeDtypeStruct((2 * rows, columns), block.dtype),
        compiler_params=pltpu.CompilerParams(vmem_limit_bytes=VMEM),
        cost_estimate=small_cost(),
        name="join",
    )(low, after, block, far)


def doubled(block, axis, bit, rank):
    size = lax.axis_size(axis)
    far = lax.ppermute(block, axis, [(i, i ^ bit) for i in range(size)])
    low = (rank & bit) == 0
    return jnp.concatenate([jnp.where(low, block, far), jnp.where(low, far, block)])


def on_device(
    enc_states,
    kv_weight,
    queries,
    out_grad,
    passage_order,
    passage_blocks,
    ret_tokens,
    ret_weight,
    question_emb,
):
    pass_dev, _, slot_len, width = enc_states.shape
    heads, pair_width = kv_weight.shape[1:]
    question_count, query_len = queries.shape[:2]
    enc_rank = lax.axis_index("enc")
    dec_rank = lax.axis_index("dec")
    ret_rank = lax.axis_index("ret")
    order_row = passage_order[0]
    blocks_row = passage_blocks[0]
    tokens = pass_dev * slot_len
    swap = [(0, 1), (1, 0)]

    rows = question_count * query_len
    packed = pack(order_row, queries.reshape(rows, HD), out_grad.reshape(rows, HD))
    gathered = lax.all_to_all(
        packed.reshape(N_ENC, pass_dev * query_len, pair_width),
        "enc",
        split_axis=0,
        concat_axis=0,
        tiled=True,
    )

    tok_rows = enc_states.reshape(tokens, width)
    key_value = project(tok_rows, kv_weight)

    own_pass = enc_rank * pass_dev + jnp.arange(pass_dev, dtype=jnp.int32)
    slot_of = jnp.sum(
        jnp.where(
            order_row[None, :] == own_pass[:, None],
            jnp.arange(order_row.shape[0], dtype=jnp.int32)[None, :],
            0,
        ),
        axis=1,
    )
    own_question = slot_of // PASS
    own_blocks = lax.dynamic_slice_in_dim(blocks_row, enc_rank * pass_dev, pass_dev)
    own_emb = jnp.sum(
        jnp.where(
            (own_question[:, None] == jnp.arange(question_count)[None, :])[..., None],
            question_emb[None],
            0.0,
        ),
        axis=1,
    )
    ret_rows = ret_tokens.reshape(tokens, ret_tokens.shape[3])
    ret_width = ret_rows.shape[1]
    pre_act = jnp.dot(ret_rows, ret_weight, preferred_element_type=F32).reshape(
        pass_dev, slot_len, ret_width
    )
    own_live = jnp.arange(slot_len, dtype=jnp.int32)[None, :] < BLK * own_blocks[:, None]
    own_length = (BLK * own_blocks).astype(F32)
    embed_own = (
        jnp.sum(jnp.where(own_live[..., None], jax.nn.gelu(pre_act), 0.0), axis=1)
        / own_length[:, None]
    )
    own_score = jnp.sum(own_emb * embed_own, axis=-1)
    score_rows = jnp.broadcast_to(
        jnp.concatenate([own_score, jnp.zeros((8 - pass_dev,), F32)])[:, None], (8, 128)
    )

    stats, late_emb = local_stats(
        own_question, own_blocks, key_value, gathered, score_rows, own_emb
    )
    mine, to_send = turn(ret_rank, stats, tok_rows)
    other = lax.ppermute(to_send, "ret", swap)
    hidden_grad = jnp.where(
        own_live[..., None], (late_emb / own_length[:, None])[:, None, :], 0.0
    )
    pre_grad = gelu_grad(pre_act, hidden_grad).astype(BF16)
    share = ret_width // N_DEC
    part_rows = lax.dynamic_slice_in_dim(ret_rows, dec_rank * share, share, axis=1)
    ret_parts = lax.dot_general(
        part_rows.reshape(pass_dev, slot_len, share),
        pre_grad,
        (((1,), (1,)), ((0,), (0,))),
        preferred_element_type=F32,
    )
    stats_all = lax.all_to_all(stats, "enc", split_axis=0, concat_axis=0, tiled=True)
    flat_a, norms, aux = back_first(
        (ret_parts, other), own_question, own_blocks, enc_rank, order_row, key_value, gathered, stats_all
    )
    far_a = lax.ppermute(flat_a, "ret", swap)
    flat_b = back_second(own_question, own_blocks, key_value, gathered, norms)
    far_b = lax.ppermute(flat_b, "ret", swap)

    turned = [
        mine.reshape(SIDE, SIDE, 128, tokens),
        other.reshape(SIDE, SIDE, 128, tokens),
    ]
    grads = [[flat_a, far_a], [flat_b, far_b]]
    at = (enc_rank // SIDE, enc_rank % SIDE)
    steps = lambda part, *ks: (at[part] + jnp.array(ks, jnp.int32)) % SIDE
    def level(after, half, bit):
        far = lax.ppermute(half, "enc", [(i, i ^ bit) for i in range(N_ENC)])
        return add_after(after, half, far)

    masses = [
        lax.ppermute(aux, "dec", [(i, (i + step) % N_DEC) for i in range(N_DEC)])
        for step in range(1, N_DEC)
    ]
    keep, give = apply_gap(
        ret_rank, aux, masses, ret_parts, N_DEC * heads * query_len, flat_b
    )
    half = add(keep, lax.ppermute(give, "ret", swap))
    a, b = far_chunk(steps(0, 2), 0, turned, grads[0], half)
    came = [(send(a, 0, 1), send(b, 0, -1))]
    half = level(a, half, 1)
    a, b = far_chunk(steps(1, 2), 1, turned, grads[1], half)
    came.append((send(a, 1, 1), send(b, 1, -1)))
    half = level(a, half, 4)
    up, down = side_chunks(steps(0, 1, 3), 0, turned, grads[0], half, came[0])
    sent = [(send(up, 0, 1), send(down, 0, -1))]
    half = level(up, half, 8)
    up, down = side_chunks(steps(1, 1, 3), 1, turned, grads[1], half, came[1])
    sent.append((send(up, 1, 1), send(down, 1, -1)))
    half = level(up, half, 2)
    own = [own_chunk(steps(0, 0), 0, turned, grads[0], up)]
    own.append(own_chunk(steps(1, 0), 1, turned, grads[1], own[0]))
    quarter = doubled(half, "ret", 1, ret_rank)
    far = lax.ppermute(quarter, "dec", [(i, i ^ 1) for i in range(N_DEC)])
    pieces, last = [], (own[1], own[1])
    for part in range(2):
        cuts = totals(at[1 - part], last, own[part], *sent[part])
        pieces.append([cuts[0]] + [send(cuts[k], 1 - part, k) for k in range(1, SIDE)])
        if part == 0:
            ret_half = joined(cuts[0], quarter, far, 1, dec_rank)
        last = (cuts[0], ret_half)
    ret_weight_grad = doubled(ret_half, "dec", 2, dec_rank)
    kv_grad = by_token(cuts[0], flat_a, flat_b).reshape(
        pass_dev, 1, slot_len, heads, pair_width
    )
    summed = first_half(ret_weight_grad, pieces[0])
    weight_total = finish(summed, pieces[1])

    return (kv_grad, weight_total, ret_weight_grad)


def solution(mesh):
    return jax.shard_map(
        on_device,
        mesh=mesh,
        in_specs=(
            P("enc", "ret", None, None),
            P(None, "dec", None),
            P("ret", None, ("dec", "enc"), None),
            P("ret", None, ("dec", "enc"), None),
            P("ret", None),
            P("ret", None),
            P("enc", "ret", None, None),
            P(),
            P("ret", None),
        ),
        out_specs=(P("enc", "ret", None, "dec", None), P(("enc", "ret"), "dec", None), P()),
        check_vma=False,
    )
```

```python
import functools

import jax
import jax.numpy as jnp
from jax import lax
from jax.experimental import pallas as pl
from jax.experimental.pallas import tpu as pltpu
from jax.sharding import PartitionSpec as P

BLK = 128
PASS = 8
N_ENC = 16
SIDE = 4
N_DEC = 4
LQ = 128
HD = 64
SLOT = 256
F32 = jnp.float32
BF16 = jnp.bfloat16
VMEM = 60 << 20


def small_cost():
    return pl.CostEstimate(flops=1 << 10, bytes_accessed=1 << 10, transcendentals=0)


def gelu_grad(pre_act, upstream):
    return jax.vjp(jax.nn.gelu, pre_act)[1](upstream)[0]


def pack_kernel(order_ref, q_ref, d_ref, o_ref):
    rows = o_ref.shape[1]
    packed = []
    for question in range(q_ref.shape[0] // rows):
        at = slice(question * rows, (question + 1) * rows)
        packed.append(
            jnp.concatenate([q_ref[at] * jnp.asarray(0.125, BF16), d_ref[at]], axis=1)
        )
    for slot in range(o_ref.shape[0]):
        o_ref[order_ref[slot]] = packed[slot // PASS]


def pack(order_row, q_rows, d_rows):
    total, head_dim = q_rows.shape
    passages = order_row.shape[0]
    return pl.pallas_call(
        pack_kernel,
        grid_spec=pltpu.PrefetchScalarGridSpec(
            num_scalar_prefetch=1,
            grid=(1,),
            in_specs=[pl.BlockSpec((total, head_dim), lambda i, o: (0, 0))] * 2,
            out_specs=pl.BlockSpec((passages, LQ, 2 * head_dim), lambda i, o: (0, 0, 0)),
        ),
        out_shape=jax.ShapeDtypeStruct((passages, LQ, 2 * head_dim), BF16),
        compiler_params=pltpu.CompilerParams(vmem_limit_bytes=VMEM),
        cost_estimate=small_cost(),
        name="pack",
    )(order_row, q_rows, d_rows)


def project_kernel(x_ref, w_ref, o_ref):
    @pl.when(pl.program_id(0) == 0)
    def _():
        o_ref[...] = jnp.zeros_like(o_ref)

    rows = x_ref[...]
    by_head = jnp.swapaxes(w_ref[...], 0, 1)
    for pair in range(by_head.shape[0] // 2):
        both = jnp.concatenate([by_head[2 * pair], by_head[2 * pair + 1]], axis=1)
        part = jnp.dot(rows, both, preferred_element_type=F32)
        o_ref[2 * pair] += part[:, :128]
        o_ref[2 * pair + 1] += part[:, 128:]


def project(tok_rows, kv_weight, depth=512):
    tokens, width = tok_rows.shape
    heads, pair_width = kv_weight.shape[1:]
    return pl.pallas_call(
        project_kernel,
        grid=(width // depth,),
        out_shape=jax.ShapeDtypeStruct((heads, tokens, pair_width), F32),
        in_specs=[
            pl.BlockSpec((tokens, depth), lambda i: (0, i)),
            pl.BlockSpec((depth, heads, pair_width), lambda i: (i, 0, 0)),
        ],
        out_specs=pl.BlockSpec((heads, tokens, pair_width), lambda i: (0, 0, 0)),
        compiler_params=pltpu.CompilerParams(vmem_limit_bytes=VMEM),
        cost_estimate=small_cost(),
        name="project",
    )(tok_rows, kv_weight)


def turn_kernel(rank_ref, after_ref, x_ref, mine_ref, send_ref):
    first = rank_ref[0] == 0
    for block in range(mine_ref.shape[0]):
        even = x_ref[:, block * 256 : block * 256 + 128].T
        odd = x_ref[:, block * 256 + 128 : block * 256 + 256].T
        mine_ref[block] = jnp.where(first, even, odd)
        send_ref[block] = jnp.where(first, odd, even)


def turn(ret_rank, after, tok_rows, per_step=8):
    tokens, width = tok_rows.shape
    half = jax.ShapeDtypeStruct((N_ENC, 128, tokens), BF16)
    return pl.pallas_call(
        turn_kernel,
        grid_spec=pltpu.PrefetchScalarGridSpec(
            num_scalar_prefetch=1,
            grid=(N_ENC // per_step,),
            in_specs=[
                pl.BlockSpec(memory_space=pl.ANY),
                pl.BlockSpec((tokens, 256 * per_step), lambda i, r: (0, i)),
            ],
            out_specs=[pl.BlockSpec((per_step, 128, tokens), lambda i, r: (i, 0, 0))] * 2,
        ),
        out_shape=[half, half],
        compiler_params=pltpu.CompilerParams(vmem_limit_bytes=VMEM),
        cost_estimate=pl.CostEstimate(
            flops=0, bytes_accessed=64 << 20, transcendentals=0
        ),
        name="turn",
    )(ret_rank.reshape(1), after, tok_rows)


def local_scores(kv_ref, qd_ref, head, passage, blocks):
    pair = kv_ref[head, passage * SLOT : (passage + 1) * SLOT, :]
    high = pair.astype(BF16)
    low = (pair - high.astype(F32)).astype(BF16)
    rows = qd_ref[head, passage * LQ : (passage + 1) * LQ, :]
    lane = lax.broadcasted_iota(jnp.int32, rows.shape, 1)
    zero = jnp.zeros_like(rows)
    stacked = jnp.concatenate(
        [jnp.where(lane < HD, rows, zero), jnp.where(lane < HD, zero, rows)], axis=0
    )
    both = lax.dot_general(
        jnp.concatenate([high, low], axis=1),
        jnp.concatenate([stacked, stacked], axis=1),
        (((1,), (1,)), ((), ())),
        preferred_element_type=F32,
    )
    scores = both[:, :LQ]
    place = lax.broadcasted_iota(jnp.int32, scores.shape, 0)
    return jnp.where(place < BLK * blocks, scores, -1e30), both[:, LQ:], stacked


def stats_kernel(
    heads, question_ref, blocks_ref, kv_ref, qd_ref, score_ref, emb_ref, o_ref, late_ref, rows_ref
):
    step = pl.program_id(0)
    per_step = kv_ref.shape[0]
    for passage in range(2):
        tops, dots = [], []
        for head in range(per_step):
            scores, prob_grad, _ = local_scores(
                kv_ref, qd_ref, head, passage, blocks_ref[passage]
            )
            top = jnp.max(scores, axis=0, keepdims=True)
            expo = jnp.exp(scores - top)
            total = jnp.sum(expo, axis=0, keepdims=True)
            tops.append(top + jnp.log(total))
            dots.append(jnp.sum(expo * prob_grad, axis=0, keepdims=True) / total)
        place = passage * heads + step * per_step
        rows_ref[pl.ds(pl.multiple_of(place, 8), per_step), :] = jnp.concatenate(tops, axis=0)
        rows_ref[pl.ds(pl.multiple_of(2 * heads + place, 8), per_step), :] = jnp.concatenate(
            dots, axis=0
        )

    @pl.when(step == pl.num_programs(0) - 1)
    def _():
        rows_ref[4 * heads :, :] = score_ref[...]
        late_ref[...] = emb_ref[...]
        o_ref[...] = jnp.broadcast_to(rows_ref[...][None], o_ref.shape)


def local_stats(own_question, own_blocks, key_value, gathered, score_rows, own_emb):
    heads, tokens, pair_width = key_value.shape
    per_step = 8
    rows = 4 * heads + 8
    return pl.pallas_call(
        functools.partial(stats_kernel, heads),
        grid_spec=pltpu.PrefetchScalarGridSpec(
            num_scalar_prefetch=2,
            grid=(heads // per_step,),
            in_specs=[
                pl.BlockSpec((per_step, tokens, pair_width), lambda i, *_: (i, 0, 0)),
                pl.BlockSpec((per_step,) + gathered.shape[1:], lambda i, *_: (i, 0, 0)),
                pl.BlockSpec((8, 128), lambda i, *_: (0, 0)),
                pl.BlockSpec(own_emb.shape, lambda i, *_: (0, 0)),
            ],
            out_specs=[
                pl.BlockSpec((N_ENC, rows, 128), lambda i, *_: (0, 0, 0)),
                pl.BlockSpec(own_emb.shape, lambda i, *_: (0, 0)),
            ],
            scratch_shapes=[pltpu.VMEM((rows, 128), F32)],
        ),
        out_shape=[
            jax.ShapeDtypeStruct((N_ENC, rows, 128), F32),
            jax.ShapeDtypeStruct(own_emb.shape, F32),
        ],
        compiler_params=pltpu.CompilerParams(vmem_limit_bytes=VMEM),
        cost_estimate=small_cost(),
        name="local_stats",
    )(own_question, own_blocks, key_value, gathered, score_rows, own_emb)


def merge_stats(heads, question_ref, own_ref, order_ref, stats_ref, norm_ref, aux_ref):
    masses, shares = [], []
    for passage in range(2):
        tops, dots, marks = [], [], []
        for slot in range(PASS):
            place = order_ref[question_ref[passage] * PASS + slot]
            owner = place // 2
            at = place - 2 * owner
            tops.append(stats_ref[owner, pl.ds(pl.multiple_of(at * heads, heads), heads), :])
            dots.append(
                stats_ref[owner, pl.ds(pl.multiple_of((2 + at) * heads, heads), heads), :]
            )
            pair = stats_ref[owner, 4 * heads : 4 * heads + 8, :]
            marks.append(jnp.where(at == 0, pair[0:1], pair[1:2]))
        top = functools.reduce(jnp.maximum, tops)
        norm = top + jnp.log(sum(jnp.exp(t - top) for t in tops))
        norm_ref[passage] = norm
        norm_ref[2 + passage] = sum(jnp.exp(t - norm) * d for t, d in zip(tops, dots))
        own = stats_ref[own_ref[0], passage * heads : (passage + 1) * heads, :]
        mass = jnp.sum(jnp.exp(own - norm), axis=0, keepdims=True)
        masses.append(jnp.broadcast_to(jnp.sum(mass, axis=1, keepdims=True), (1, 128)))
        best = functools.reduce(jnp.maximum, marks)
        mark = stats_ref[own_ref[0], 4 * heads : 4 * heads + 8, :][passage : passage + 1]
        shares.append(jnp.exp(mark - best) / sum(jnp.exp(m - best) for m in marks))
    aux_ref[...] = jnp.concatenate(masses + shares + [jnp.zeros((4, 128), F32)], axis=0)


def back_heads(part, question_ref, blocks_ref, kv_ref, qd_ref, norm_ref, flat_ref):
    per_step = kv_ref.shape[0]
    first = part * 8 + pl.program_id(0) * per_step
    for passage in range(2):
        for head in range(per_step):
            scores, prob_grad, stacked = local_scores(
                kv_ref, qd_ref, head, passage, blocks_ref[passage]
            )
            norm = norm_ref[passage, pl.ds(first + head, 1), :]
            dot = norm_ref[2 + passage, pl.ds(first + head, 1), :]
            probs = jnp.exp(scores - norm)
            score_grad = probs * (prob_grad - dot)
            left = jnp.concatenate([score_grad, probs], axis=1).astype(BF16)
            grad = jnp.dot(left, stacked, preferred_element_type=F32).astype(BF16)
            flat_ref[
                passage * SLOT : (passage + 1) * SLOT, head * 128 : (head + 1) * 128
            ] = grad


def back_first_kernel(
    heads,
    question_ref,
    blocks_ref,
    own_ref,
    order_ref,
    after_ref,
    also_ref,
    kv_ref,
    qd_ref,
    stats_ref,
    flat_ref,
    norm_ref,
    aux_ref,
):
    @pl.when(pl.program_id(0) == 0)
    def _():
        merge_stats(heads, question_ref, own_ref, order_ref, stats_ref, norm_ref, aux_ref)

    back_heads(0, question_ref, blocks_ref, kv_ref, qd_ref, norm_ref, flat_ref)


def back_second_kernel(question_ref, blocks_ref, kv_ref, qd_ref, norm_ref, flat_ref):
    back_heads(1, question_ref, blocks_ref, kv_ref, qd_ref, norm_ref, flat_ref)


BACK_COST = pl.CostEstimate(flops=0, bytes_accessed=32 << 20, transcendentals=0)


def back_specs(key_value, gathered, part, per_step):
    base = part * 8 // per_step
    tokens, pair_width = key_value.shape[1:]
    return [
        pl.BlockSpec((per_step, tokens, pair_width), lambda i, *_: (base + i, 0, 0)),
        pl.BlockSpec((per_step,) + gathered.shape[1:], lambda i, *_: (base + i, 0, 0)),
    ]


def back_first(after, own_question, own_blocks, enc_rank, order_row, key_value, gathered, stats, per_step=4):
    heads, tokens, pair_width = key_value.shape
    return pl.pallas_call(
        functools.partial(back_first_kernel, heads),
        grid_spec=pltpu.PrefetchScalarGridSpec(
            num_scalar_prefetch=4,
            grid=(8 // per_step,),
            in_specs=[pl.BlockSpec(memory_space=pl.ANY)] * 2
            + back_specs(key_value, gathered, 0, per_step)
            + [pl.BlockSpec(stats.shape, lambda i, *_: (0, 0, 0))],
            out_specs=[
                pl.BlockSpec((tokens, per_step * pair_width), lambda i, *_: (0, i)),
                pl.BlockSpec((4, heads, 128), lambda i, *_: (0, 0, 0)),
                pl.BlockSpec((8, 128), lambda i, *_: (0, 0)),
            ],
        ),
        out_shape=[
            jax.ShapeDtypeStruct((tokens, 8 * pair_width), BF16),
            jax.ShapeDtypeStruct((4, heads, 128), F32),
            jax.ShapeDtypeStruct((8, 128), F32),
        ],
        compiler_params=pltpu.CompilerParams(vmem_limit_bytes=VMEM),
        cost_estimate=BACK_COST,
        name="back_first",
    )(own_question, own_blocks, enc_rank.reshape(1), order_row, *after, key_value, gathered, stats)


def back_second(own_question, own_blocks, key_value, gathered, norms, per_step=4):
    heads, tokens, pair_width = key_value.shape
    return pl.pallas_call(
        back_second_kernel,
        grid_spec=pltpu.PrefetchScalarGridSpec(
            num_scalar_prefetch=2,
            grid=(8 // per_step,),
            in_specs=back_specs(key_value, gathered, 1, per_step)
            + [pl.BlockSpec(norms.shape, lambda i, *_: (0, 0, 0))],
            out_specs=pl.BlockSpec((tokens, per_step * pair_width), lambda i, *_: (0, i)),
        ),
        out_shape=jax.ShapeDtypeStruct((tokens, 8 * pair_width), BF16),
        compiler_params=pltpu.CompilerParams(vmem_limit_bytes=VMEM),
        cost_estimate=BACK_COST,
        name="back_second",
    )(own_question, own_blocks, key_value, gathered, norms)


def product(near_ref, far_ref, own_ref, other_ref):
    rows, depth = SIDE * 128, near_ref.shape[-1]
    total = jnp.dot(near_ref[...].reshape(rows, depth), own_ref[...], preferred_element_type=F32)
    return total + jnp.dot(
        far_ref[...].reshape(rows, depth), other_ref[...], preferred_element_type=F32
    )


def chunk_spec(part, tokens, which):
    if part == 0:
        return pl.BlockSpec((1, SIDE, 128, tokens), lambda i, w: (w[which], 0, 0, 0))
    return pl.BlockSpec((SIDE, 1, 128, tokens), lambda i, w: (0, w[which], 0, 0))


def ordered(kernel, which_ref, after_ref, also_ref, *refs):
    kernel(which_ref, *refs)


def chunk_call(
    kernel, name, which, part, turned, grads, after, extra, extra_specs, out_specs, out_shape
):
    after = after if isinstance(after, tuple) else (after, after)
    tokens, columns = grads[0].shape
    half = pl.BlockSpec((tokens, columns // 2), lambda i, w: (0, i))
    chunks = which.shape[0]
    turned_specs, turned_args = [], []
    for index in range(chunks):
        turned_specs += [chunk_spec(part, tokens, index)] * 2
        turned_args += turned
    return pl.pallas_call(
        functools.partial(ordered, kernel),
        grid_spec=pltpu.PrefetchScalarGridSpec(
            num_scalar_prefetch=1,
            grid=(2,),
            in_specs=[pl.BlockSpec(memory_space=pl.ANY)] * 2
            + turned_specs
            + [half, half]
            + extra_specs,
            out_specs=out_specs,
        ),
        out_shape=out_shape,
        compiler_params=pltpu.CompilerParams(vmem_limit_bytes=VMEM),
        cost_estimate=small_cost(),
        name=name,
    )(which, *after, *turned_args, *grads, *extra)


def far_kernel(which_ref, near_ref, far_ref, own_ref, other_ref, a_ref, b_ref):
    total = product(near_ref, far_ref, own_ref, other_ref).astype(BF16)

    @pl.when(pl.program_id(0) == 0)
    def _():
        a_ref[...] = total

    @pl.when(pl.program_id(0) == 1)
    def _():
        b_ref[...] = total


def far_chunk(which, part, turned, grads, after):
    rows, columns = SIDE * 128, grads[0].shape[1] // 2
    half = jax.ShapeDtypeStruct((rows, columns), BF16)
    half_spec = pl.BlockSpec((rows, columns), lambda i, w: (0, 0))
    return chunk_call(
        far_kernel, "far_chunk", which, part, turned, grads, after, [], [], [half_spec] * 2, [half] * 2
    )


def own_kernel(which_ref, near_ref, far_ref, own_ref, other_ref, o_ref):
    o_ref[0] = product(near_ref, far_ref, own_ref, other_ref).astype(BF16)


def own_chunk(which, part, turned, grads, after):
    rows, columns = SIDE * 128, grads[0].shape[1] // 2
    return chunk_call(
        own_kernel,
        "own_chunk",
        which,
        part,
        turned,
        grads,
        after,
        [],
        [],
        pl.BlockSpec((1, rows, columns), lambda i, w: (i, 0, 0)),
        jax.ShapeDtypeStruct((2, rows, columns), BF16),
    )


def side_kernel(
    which_ref, up_near, up_far, down_near, down_far, own_ref, other_ref, a_ref, b_ref, up_ref, down_ref
):
    first = pl.program_id(0) == 0
    zero = jnp.zeros(a_ref.shape, F32)
    up = product(up_near, up_far, own_ref, other_ref)
    up_ref[0] = (up + jnp.where(first, a_ref[...].astype(F32), zero)).astype(BF16)
    down = product(down_near, down_far, own_ref, other_ref)
    down_ref[0] = (down + jnp.where(first, zero, b_ref[...].astype(F32))).astype(BF16)


def side_chunks(which, part, turned, grads, after, came):
    rows, columns = SIDE * 128, grads[0].shape[1] // 2
    both = jax.ShapeDtypeStruct((2, rows, columns), BF16)
    out = pl.BlockSpec((1, rows, columns), lambda i, w: (i, 0, 0))
    full = pl.BlockSpec((rows, columns), lambda i, w: (0, 0))
    return chunk_call(
        side_kernel, "side_chunks", which, part, turned, grads, after, list(came), [full, full], [out, out], [both, both]
    )


def total_kernel(which_ref, after_ref, also_ref, own_ref, up_ref, down_ref, *out_refs):
    total = own_ref[...].astype(F32) + up_ref[...].astype(F32) + down_ref[...].astype(F32)
    for step, ref in enumerate(out_refs):

        @pl.when(pl.program_id(0) == step)
        def _():
            ref[...] = total[:, 0].astype(BF16)


def totals(first, after, own, up, down):
    columns = own.shape[-1]
    cut = lambda a: a.reshape(2, SIDE, 128, columns)
    block = pl.BlockSpec((2, 1, 128, columns), lambda i, w: (0, (w[0] + i) % SIDE, 0, 0))
    out = pl.BlockSpec((2, 128, columns), lambda i, w: (0, 0, 0))
    return pl.pallas_call(
        total_kernel,
        grid_spec=pltpu.PrefetchScalarGridSpec(
            num_scalar_prefetch=1,
            grid=(SIDE,),
            in_specs=[pl.BlockSpec(memory_space=pl.ANY)] * 2 + [block] * 3,
            out_specs=[out] * SIDE,
        ),
        out_shape=[jax.ShapeDtypeStruct((2, 128, columns), BF16)] * SIDE,
        compiler_params=pltpu.CompilerParams(vmem_limit_bytes=VMEM),
        cost_estimate=small_cost(),
        name="totals",
    )(first.reshape(1), *after, cut(own), cut(up), cut(down))


def gather_terms(refs):
    return sum(r[...].astype(F32) for r in refs).astype(BF16)


def first_kernel(after_ref, *refs):
    refs[-1][...] = gather_terms(refs[:-1])


def first_half(after, pieces):
    block = pl.BlockSpec(pieces[0].shape, lambda: (0, 0, 0))
    return pl.pallas_call(
        first_kernel,
        in_specs=[pl.BlockSpec(memory_space=pl.ANY)] + [block] * len(pieces),
        out_specs=block,
        out_shape=jax.ShapeDtypeStruct(pieces[0].shape, BF16),
        compiler_params=pltpu.CompilerParams(vmem_limit_bytes=VMEM),
        cost_estimate=small_cost(),
        name="first_half",
    )(after, *pieces)


def finish_kernel(first_ref, *refs):
    heads = []
    for total in (first_ref[...], gather_terms(refs[:-1])):
        for half in range(2):
            for head in range(4):
                heads.append(total[half, :, head * 128 : (head + 1) * 128])
    refs[-1][...] = jnp.swapaxes(jnp.stack(heads), 0, 1)


def finish(first, pieces):
    return pl.pallas_call(
        finish_kernel,
        out_shape=jax.ShapeDtypeStruct((128, 16, 128), BF16),
        compiler_params=pltpu.CompilerParams(vmem_limit_bytes=VMEM),
        cost_estimate=small_cost(),
        name="finish",
    )(first, *pieces)


def by_token_kernel(after_ref, a_ref, b_ref, o_ref):
    heads = [ref[:, h * 128 : (h + 1) * 128] for ref in (a_ref, b_ref) for h in range(8)]
    o_ref[...] = jnp.swapaxes(jnp.stack(heads), 0, 1)


def by_token(after, a, b, rows=128):
    tokens, columns = a.shape
    block = pl.BlockSpec((rows, columns), lambda i: (i, 0))
    return pl.pallas_call(
        by_token_kernel,
        grid=(tokens // rows,),
        in_specs=[pl.BlockSpec(memory_space=pl.ANY), block, block],
        out_specs=pl.BlockSpec((rows, 16, 128), lambda i: (i, 0, 0)),
        out_shape=jax.ShapeDtypeStruct((tokens, 16, 128), BF16),
        compiler_params=pltpu.CompilerParams(vmem_limit_bytes=VMEM),
        cost_estimate=small_cost(),
        name="by_token",
    )(after, a, b)


def add_after(after, a, b):
    a, after = lax.optimization_barrier((a, after))
    return add(a, b)


def gap_kernel(heads_rows, rank_ref, aux_ref, m1_ref, m2_ref, m3_ref, part_ref, gate_ref, keep_ref, give_ref):
    rows = keep_ref.shape[0]
    mass = (aux_ref[0:2] + m1_ref[0:2]) + (m2_ref[0:2] + m3_ref[0:2])
    gap = aux_ref[2:4] - mass / heads_rows
    rank = rank_ref[0]

    def at(place):
        here = pl.ds(pl.multiple_of(place * rows, 8), rows)
        return gap[0:1, 0:1] * part_ref[0, here, :] + gap[1:2, 0:1] * part_ref[1, here, :]

    keep_ref[...] = at(rank)
    give_ref[...] = at(1 - rank).astype(BF16)


def apply_gap(ret_rank, aux, masses, parts, heads_rows, gate):
    _, rows, columns = parts.shape
    whole = lambda *shape: pl.BlockSpec(shape, lambda i, r: (0,) * len(shape))
    return pl.pallas_call(
        functools.partial(gap_kernel, float(heads_rows)),
        grid_spec=pltpu.PrefetchScalarGridSpec(
            num_scalar_prefetch=1,
            grid=(1,),
            in_specs=[whole(8, 128)] * 4
            + [whole(2, rows, columns), pl.BlockSpec(memory_space=pl.ANY)],
            out_specs=[whole(rows // 2, columns)] * 2,
        ),
        out_shape=[
            jax.ShapeDtypeStruct((rows // 2, columns), F32),
            jax.ShapeDtypeStruct((rows // 2, columns), BF16),
        ],
        compiler_params=pltpu.CompilerParams(vmem_limit_bytes=VMEM),
        cost_estimate=small_cost(),
        name="apply_gap",
    )(ret_rank.reshape(1), aux, *masses, parts, gate)


def ring_pairs(axis, step):
    pairs = []
    for x in range(SIDE):
        for y in range(SIDE):
            to = ((x + step) % SIDE, y) if axis == 0 else (x, (y + step) % SIDE)
            pairs.append((x * SIDE + y, to[0] * SIDE + to[1]))
    return pairs


def send(value, axis, step):
    return lax.ppermute(value, "enc", ring_pairs(axis, step))


def add(*terms):
    return sum(t.astype(F32) for t in terms).astype(BF16)


def join_kernel(low_ref, after_ref, own_ref, far_ref, o_ref):
    rows = own_ref.shape[0]
    low = low_ref[0] == 1
    own, far = own_ref[...], far_ref[...]
    o_ref[:rows] = jnp.where(low, own, far)
    o_ref[rows:] = jnp.where(low, far, own)


def joined(after, block, far, bit, rank):
    rows, columns = block.shape
    low = ((rank & bit) == 0).astype(jnp.int32).reshape(1)
    half = pl.BlockSpec((rows, columns), lambda i, r: (0, 0))
    return pl.pallas_call(
        join_kernel,
        grid_spec=pltpu.PrefetchScalarGridSpec(
            num_scalar_prefetch=1,
            grid=(1,),
            in_specs=[pl.BlockSpec(memory_space=pl.ANY), half, half],
            out_specs=pl.BlockSpec((2 * rows, columns), lambda i, r: (0, 0)),
        ),
        out_shape=jax.ShapeDtypeStruct((2 * rows, columns), block.dtype),
        compiler_params=pltpu.CompilerParams(vmem_limit_bytes=VMEM),
        cost_estimate=small_cost(),
        name="join",
    )(low, after, block, far)


def doubled(block, axis, bit, rank):
    size = lax.axis_size(axis)
    far = lax.ppermute(block, axis, [(i, i ^ bit) for i in range(size)])
    low = (rank & bit) == 0
    return jnp.concatenate([jnp.where(low, block, far), jnp.where(low, far, block)])


def on_device(
    enc_states,
    kv_weight,
    queries,
    out_grad,
    passage_order,
    passage_blocks,
    ret_tokens,
    ret_weight,
    question_emb,
):
    pass_dev, _, slot_len, width = enc_states.shape
    heads, pair_width = kv_weight.shape[1:]
    question_count, query_len = queries.shape[:2]
    enc_rank = lax.axis_index("enc")
    dec_rank = lax.axis_index("dec")
    ret_rank = lax.axis_index("ret")
    order_row = passage_order[0]
    blocks_row = passage_blocks[0]
    tokens = pass_dev * slot_len
    swap = [(0, 1), (1, 0)]

    rows = question_count * query_len
    packed = pack(order_row, queries.reshape(rows, HD), out_grad.reshape(rows, HD))
    gathered = lax.all_to_all(
        packed.reshape(N_ENC, pass_dev * query_len, pair_width),
        "enc",
        split_axis=0,
        concat_axis=0,
        tiled=True,
    )

    tok_rows = enc_states.reshape(tokens, width)
    key_value = project(tok_rows, kv_weight)

    own_pass = enc_rank * pass_dev + jnp.arange(pass_dev, dtype=jnp.int32)
    slot_of = jnp.sum(
        jnp.where(
            order_row[None, :] == own_pass[:, None],
            jnp.arange(order_row.shape[0], dtype=jnp.int32)[None, :],
            0,
        ),
        axis=1,
    )
    own_question = slot_of // PASS
    own_blocks = lax.dynamic_slice_in_dim(blocks_row, enc_rank * pass_dev, pass_dev)
    own_emb = jnp.sum(
        jnp.where(
            (own_question[:, None] == jnp.arange(question_count)[None, :])[..., None],
            question_emb[None],
            0.0,
        ),
        axis=1,
    )
    ret_rows = ret_tokens.reshape(tokens, ret_tokens.shape[3])
    ret_width = ret_rows.shape[1]
    pre_act = jnp.dot(ret_rows, ret_weight, preferred_element_type=F32).reshape(
        pass_dev, slot_len, ret_width
    )
    own_live = jnp.arange(slot_len, dtype=jnp.int32)[None, :] < BLK * own_blocks[:, None]
    own_length = (BLK * own_blocks).astype(F32)
    embed_own = (
        jnp.sum(jnp.where(own_live[..., None], jax.nn.gelu(pre_act), 0.0), axis=1)
        / own_length[:, None]
    )
    own_score = jnp.sum(own_emb * embed_own, axis=-1)
    score_rows = jnp.broadcast_to(
        jnp.concatenate([own_score, jnp.zeros((8 - pass_dev,), F32)])[:, None], (8, 128)
    )

    stats, late_emb = local_stats(
        own_question, own_blocks, key_value, gathered, score_rows, own_emb
    )
    mine, to_send = turn(ret_rank, stats, tok_rows)
    other = lax.ppermute(to_send, "ret", swap)
    hidden_grad = jnp.where(
        own_live[..., None], (late_emb / own_length[:, None])[:, None, :], 0.0
    )
    pre_grad = gelu_grad(pre_act, hidden_grad).astype(BF16)
    share = ret_width // N_DEC
    part_rows = lax.dynamic_slice_in_dim(ret_rows, dec_rank * share, share, axis=1)
    ret_parts = lax.dot_general(
        part_rows.reshape(pass_dev, slot_len, share),
        pre_grad,
        (((1,), (1,)), ((0,), (0,))),
        preferred_element_type=F32,
    )
    stats_all = lax.all_to_all(stats, "enc", split_axis=0, concat_axis=0, tiled=True)
    flat_a, norms, aux = back_first(
        (ret_parts, other), own_question, own_blocks, enc_rank, order_row, key_value, gathered, stats_all
    )
    far_a = lax.ppermute(flat_a, "ret", swap)
    flat_b = back_second(own_question, own_blocks, key_value, gathered, norms)
    far_b = lax.ppermute(flat_b, "ret", swap)

    turned = [
        mine.reshape(SIDE, SIDE, 128, tokens),
        other.reshape(SIDE, SIDE, 128, tokens),
    ]
    grads = [[flat_a, far_a], [flat_b, far_b]]
    at = (enc_rank // SIDE, enc_rank % SIDE)
    steps = lambda part, *ks: (at[part] + jnp.array(ks, jnp.int32)) % SIDE
    def level(after, half, bit):
        far = lax.ppermute(half, "enc", [(i, i ^ bit) for i in range(N_ENC)])
        return add_after(after, half, far)

    masses = [
        lax.ppermute(aux, "dec", [(i, (i + step) % N_DEC) for i in range(N_DEC)])
        for step in range(1, N_DEC)
    ]
    keep, give = apply_gap(
        ret_rank, aux, masses, ret_parts, N_DEC * heads * query_len, flat_b
    )
    half = add(keep, lax.ppermute(give, "ret", swap))
    a, b = far_chunk(steps(0, 2), 0, turned, grads[0], half)
    came = [(send(a, 0, 1), send(b, 0, -1))]
    half = level(a, half, 1)
    a, b = far_chunk(steps(1, 2), 1, turned, grads[1], half)
    came.append((send(a, 1, 1), send(b, 1, -1)))
    half = level(a, half, 4)
    up, down = side_chunks(steps(0, 1, 3), 0, turned, grads[0], half, came[0])
    sent = [(send(up, 0, 1), send(down, 0, -1))]
    half = level(up, half, 8)
    up, down = side_chunks(steps(1, 1, 3), 1, turned, grads[1], half, came[1])
    sent.append((send(up, 1, 1), send(down, 1, -1)))
    half = level(up, half, 2)
    own = [own_chunk(steps(0, 0), 0, turned, grads[0], up)]
    own.append(own_chunk(steps(1, 0), 1, turned, grads[1], own[0]))
    quarter = doubled(half, "ret", 1, ret_rank)
    far = lax.ppermute(quarter, "dec", [(i, i ^ 1) for i in range(N_DEC)])
    pieces, last = [], (own[1], own[1])
    for part in range(2):
        cuts = totals(at[1 - part], last, own[part], *sent[part])
        pieces.append([cuts[0]] + [send(cuts[k], 1 - part, k) for k in range(1, SIDE)])
        if part == 0:
            ret_half = joined(cuts[0], quarter, far, 1, dec_rank)
            by_tokens = by_token(cuts[0], flat_a, flat_b)
        last = (by_tokens, ret_half)
    ret_weight_grad = doubled(ret_half, "dec", 2, dec_rank)
    kv_grad = by_tokens.reshape(
        pass_dev, 1, slot_len, heads, pair_width
    )
    summed = first_half(ret_weight_grad, pieces[0])
    weight_total = finish(summed, pieces[1])

    return (kv_grad, weight_total, ret_weight_grad)


def solution(mesh):
    return jax.shard_map(
        on_device,
        mesh=mesh,
        in_specs=(
            P("enc", "ret", None, None),
            P(None, "dec", None),
            P("ret", None, ("dec", "enc"), None),
            P("ret", None, ("dec", "enc"), None),
            P("ret", None),
            P("ret", None),
            P("enc", "ret", None, None),
            P(),
            P("ret", None),
        ),
        out_specs=(P("enc", "ret", None, "dec", None), P(("enc", "ret"), "dec", None), P()),
        check_vma=False,
    )
```

```python
import functools

import jax
import jax.numpy as jnp
from jax import lax
from jax.experimental import pallas as pl
from jax.experimental.pallas import tpu as pltpu
from jax.sharding import PartitionSpec as P

BLK = 128
PASS = 8
N_ENC = 16
SIDE = 4
N_DEC = 4
LQ = 128
HD = 64
SLOT = 256
F32 = jnp.float32
BF16 = jnp.bfloat16
VMEM = 60 << 20


def small_cost():
    return pl.CostEstimate(flops=1 << 10, bytes_accessed=1 << 10, transcendentals=0)


def gelu_grad(pre_act, upstream):
    return jax.vjp(jax.nn.gelu, pre_act)[1](upstream)[0]


def pack_kernel(order_ref, q_ref, d_ref, o_ref):
    rows = o_ref.shape[1]
    packed = []
    for question in range(q_ref.shape[0] // rows):
        at = slice(question * rows, (question + 1) * rows)
        packed.append(
            jnp.concatenate([q_ref[at] * jnp.asarray(0.125, BF16), d_ref[at]], axis=1)
        )
    for slot in range(o_ref.shape[0]):
        o_ref[order_ref[slot]] = packed[slot // PASS]


def pack(order_row, q_rows, d_rows):
    total, head_dim = q_rows.shape
    passages = order_row.shape[0]
    return pl.pallas_call(
        pack_kernel,
        grid_spec=pltpu.PrefetchScalarGridSpec(
            num_scalar_prefetch=1,
            grid=(1,),
            in_specs=[pl.BlockSpec((total, head_dim), lambda i, o: (0, 0))] * 2,
            out_specs=pl.BlockSpec((passages, LQ, 2 * head_dim), lambda i, o: (0, 0, 0)),
        ),
        out_shape=jax.ShapeDtypeStruct((passages, LQ, 2 * head_dim), BF16),
        compiler_params=pltpu.CompilerParams(vmem_limit_bytes=VMEM),
        cost_estimate=small_cost(),
        name="pack",
    )(order_row, q_rows, d_rows)


def project_kernel(x_ref, w_ref, o_ref):
    @pl.when(pl.program_id(0) == 0)
    def _():
        o_ref[...] = jnp.zeros_like(o_ref)

    rows = x_ref[...]
    by_head = jnp.swapaxes(w_ref[...], 0, 1)
    for pair in range(by_head.shape[0] // 2):
        both = jnp.concatenate([by_head[2 * pair], by_head[2 * pair + 1]], axis=1)
        part = jnp.dot(rows, both, preferred_element_type=F32)
        o_ref[2 * pair] += part[:, :128]
        o_ref[2 * pair + 1] += part[:, 128:]


def project(tok_rows, kv_weight, depth=1024):
    tokens, width = tok_rows.shape
    heads, pair_width = kv_weight.shape[1:]
    return pl.pallas_call(
        project_kernel,
        grid=(width // depth,),
        out_shape=jax.ShapeDtypeStruct((heads, tokens, pair_width), F32),
        in_specs=[
            pl.BlockSpec((tokens, depth), lambda i: (0, i)),
            pl.BlockSpec((depth, heads, pair_width), lambda i: (i, 0, 0)),
        ],
        out_specs=pl.BlockSpec((heads, tokens, pair_width), lambda i: (0, 0, 0)),
        compiler_params=pltpu.CompilerParams(vmem_limit_bytes=VMEM),
        cost_estimate=small_cost(),
        name="project",
    )(tok_rows, kv_weight)


def turn_kernel(rank_ref, after_ref, x_ref, mine_ref, send_ref):
    first = rank_ref[0] == 0
    for block in range(mine_ref.shape[0]):
        even = x_ref[:, block * 256 : block * 256 + 128].T
        odd = x_ref[:, block * 256 + 128 : block * 256 + 256].T
        mine_ref[block] = jnp.where(first, even, odd)
        send_ref[block] = jnp.where(first, odd, even)


def turn(ret_rank, after, tok_rows, per_step=8):
    tokens, width = tok_rows.shape
    half = jax.ShapeDtypeStruct((N_ENC, 128, tokens), BF16)
    return pl.pallas_call(
        turn_kernel,
        grid_spec=pltpu.PrefetchScalarGridSpec(
            num_scalar_prefetch=1,
            grid=(N_ENC // per_step,),
            in_specs=[
                pl.BlockSpec(memory_space=pl.ANY),
                pl.BlockSpec((tokens, 256 * per_step), lambda i, r: (0, i)),
            ],
            out_specs=[pl.BlockSpec((per_step, 128, tokens), lambda i, r: (i, 0, 0))] * 2,
        ),
        out_shape=[half, half],
        compiler_params=pltpu.CompilerParams(vmem_limit_bytes=VMEM),
        cost_estimate=pl.CostEstimate(
            flops=0, bytes_accessed=64 << 20, transcendentals=0
        ),
        name="turn",
    )(ret_rank.reshape(1), after, tok_rows)


def local_scores(kv_ref, qd_ref, head, passage, blocks):
    pair = kv_ref[head, passage * SLOT : (passage + 1) * SLOT, :]
    high = pair.astype(BF16)
    low = (pair - high.astype(F32)).astype(BF16)
    rows = qd_ref[head, passage * LQ : (passage + 1) * LQ, :]
    lane = lax.broadcasted_iota(jnp.int32, rows.shape, 1)
    zero = jnp.zeros_like(rows)
    stacked = jnp.concatenate(
        [jnp.where(lane < HD, rows, zero), jnp.where(lane < HD, zero, rows)], axis=0
    )
    both = lax.dot_general(
        jnp.concatenate([high, low], axis=1),
        jnp.concatenate([stacked, stacked], axis=1),
        (((1,), (1,)), ((), ())),
        preferred_element_type=F32,
    )
    scores = both[:, :LQ]
    place = lax.broadcasted_iota(jnp.int32, scores.shape, 0)
    return jnp.where(place < BLK * blocks, scores, -1e30), both[:, LQ:], stacked


def stats_kernel(
    heads, question_ref, blocks_ref, kv_ref, qd_ref, score_ref, emb_ref, o_ref, late_ref, rows_ref
):
    step = pl.program_id(0)
    per_step = kv_ref.shape[0]
    for passage in range(2):
        tops, dots = [], []
        for head in range(per_step):
            scores, prob_grad, _ = local_scores(
                kv_ref, qd_ref, head, passage, blocks_ref[passage]
            )
            top = jnp.max(scores, axis=0, keepdims=True)
            expo = jnp.exp(scores - top)
            total = jnp.sum(expo, axis=0, keepdims=True)
            tops.append(top + jnp.log(total))
            dots.append(jnp.sum(expo * prob_grad, axis=0, keepdims=True) / total)
        place = passage * heads + step * per_step
        rows_ref[pl.ds(pl.multiple_of(place, 8), per_step), :] = jnp.concatenate(tops, axis=0)
        rows_ref[pl.ds(pl.multiple_of(2 * heads + place, 8), per_step), :] = jnp.concatenate(
            dots, axis=0
        )

    @pl.when(step == pl.num_programs(0) - 1)
    def _():
        rows_ref[4 * heads :, :] = score_ref[...]
        late_ref[...] = emb_ref[...]
        o_ref[...] = jnp.broadcast_to(rows_ref[...][None], o_ref.shape)


def local_stats(own_question, own_blocks, key_value, gathered, score_rows, own_emb):
    heads, tokens, pair_width = key_value.shape
    per_step = 8
    rows = 4 * heads + 8
    return pl.pallas_call(
        functools.partial(stats_kernel, heads),
        grid_spec=pltpu.PrefetchScalarGridSpec(
            num_scalar_prefetch=2,
            grid=(heads // per_step,),
            in_specs=[
                pl.BlockSpec((per_step, tokens, pair_width), lambda i, *_: (i, 0, 0)),
                pl.BlockSpec((per_step,) + gathered.shape[1:], lambda i, *_: (i, 0, 0)),
                pl.BlockSpec((8, 128), lambda i, *_: (0, 0)),
                pl.BlockSpec(own_emb.shape, lambda i, *_: (0, 0)),
            ],
            out_specs=[
                pl.BlockSpec((N_ENC, rows, 128), lambda i, *_: (0, 0, 0)),
                pl.BlockSpec(own_emb.shape, lambda i, *_: (0, 0)),
            ],
            scratch_shapes=[pltpu.VMEM((rows, 128), F32)],
        ),
        out_shape=[
            jax.ShapeDtypeStruct((N_ENC, rows, 128), F32),
            jax.ShapeDtypeStruct(own_emb.shape, F32),
        ],
        compiler_params=pltpu.CompilerParams(vmem_limit_bytes=VMEM),
        cost_estimate=small_cost(),
        name="local_stats",
    )(own_question, own_blocks, key_value, gathered, score_rows, own_emb)


def merge_stats(heads, question_ref, own_ref, order_ref, stats_ref, norm_ref, aux_ref):
    masses, shares = [], []
    for passage in range(2):
        tops, dots, marks = [], [], []
        for slot in range(PASS):
            place = order_ref[question_ref[passage] * PASS + slot]
            owner = place // 2
            at = place - 2 * owner
            tops.append(stats_ref[owner, pl.ds(pl.multiple_of(at * heads, heads), heads), :])
            dots.append(
                stats_ref[owner, pl.ds(pl.multiple_of((2 + at) * heads, heads), heads), :]
            )
            pair = stats_ref[owner, 4 * heads : 4 * heads + 8, :]
            marks.append(jnp.where(at == 0, pair[0:1], pair[1:2]))
        top = functools.reduce(jnp.maximum, tops)
        norm = top + jnp.log(sum(jnp.exp(t - top) for t in tops))
        norm_ref[passage] = norm
        norm_ref[2 + passage] = sum(jnp.exp(t - norm) * d for t, d in zip(tops, dots))
        own = stats_ref[own_ref[0], passage * heads : (passage + 1) * heads, :]
        mass = jnp.sum(jnp.exp(own - norm), axis=0, keepdims=True)
        masses.append(jnp.broadcast_to(jnp.sum(mass, axis=1, keepdims=True), (1, 128)))
        best = functools.reduce(jnp.maximum, marks)
        mark = stats_ref[own_ref[0], 4 * heads : 4 * heads + 8, :][passage : passage + 1]
        shares.append(jnp.exp(mark - best) / sum(jnp.exp(m - best) for m in marks))
    aux_ref[...] = jnp.concatenate(masses + shares + [jnp.zeros((4, 128), F32)], axis=0)


def back_heads(part, question_ref, blocks_ref, kv_ref, qd_ref, norm_ref, flat_ref):
    per_step = kv_ref.shape[0]
    first = part * 8 + pl.program_id(0) * per_step
    for passage in range(2):
        for head in range(per_step):
            scores, prob_grad, stacked = local_scores(
                kv_ref, qd_ref, head, passage, blocks_ref[passage]
            )
            norm = norm_ref[passage, pl.ds(first + head, 1), :]
            dot = norm_ref[2 + passage, pl.ds(first + head, 1), :]
            probs = jnp.exp(scores - norm)
            score_grad = probs * (prob_grad - dot)
            left = jnp.concatenate([score_grad, probs], axis=1).astype(BF16)
            grad = jnp.dot(left, stacked, preferred_element_type=F32).astype(BF16)
            flat_ref[
                passage * SLOT : (passage + 1) * SLOT, head * 128 : (head + 1) * 128
            ] = grad


def back_first_kernel(
    heads,
    question_ref,
    blocks_ref,
    own_ref,
    order_ref,
    after_ref,
    also_ref,
    kv_ref,
    qd_ref,
    stats_ref,
    flat_ref,
    norm_ref,
    aux_ref,
):
    @pl.when(pl.program_id(0) == 0)
    def _():
        merge_stats(heads, question_ref, own_ref, order_ref, stats_ref, norm_ref, aux_ref)

    back_heads(0, question_ref, blocks_ref, kv_ref, qd_ref, norm_ref, flat_ref)


def back_second_kernel(question_ref, blocks_ref, kv_ref, qd_ref, norm_ref, flat_ref):
    back_heads(1, question_ref, blocks_ref, kv_ref, qd_ref, norm_ref, flat_ref)


BACK_COST = pl.CostEstimate(flops=0, bytes_accessed=32 << 20, transcendentals=0)


def back_specs(key_value, gathered, part, per_step):
    base = part * 8 // per_step
    tokens, pair_width = key_value.shape[1:]
    return [
        pl.BlockSpec((per_step, tokens, pair_width), lambda i, *_: (base + i, 0, 0)),
        pl.BlockSpec((per_step,) + gathered.shape[1:], lambda i, *_: (base + i, 0, 0)),
    ]


def back_first(after, own_question, own_blocks, enc_rank, order_row, key_value, gathered, stats, per_step=4):
    heads, tokens, pair_width = key_value.shape
    return pl.pallas_call(
        functools.partial(back_first_kernel, heads),
        grid_spec=pltpu.PrefetchScalarGridSpec(
            num_scalar_prefetch=4,
            grid=(8 // per_step,),
            in_specs=[pl.BlockSpec(memory_space=pl.ANY)] * 2
            + back_specs(key_value, gathered, 0, per_step)
            + [pl.BlockSpec(stats.shape, lambda i, *_: (0, 0, 0))],
            out_specs=[
                pl.BlockSpec((tokens, per_step * pair_width), lambda i, *_: (0, i)),
                pl.BlockSpec((4, heads, 128), lambda i, *_: (0, 0, 0)),
                pl.BlockSpec((8, 128), lambda i, *_: (0, 0)),
            ],
        ),
        out_shape=[
            jax.ShapeDtypeStruct((tokens, 8 * pair_width), BF16),
            jax.ShapeDtypeStruct((4, heads, 128), F32),
            jax.ShapeDtypeStruct((8, 128), F32),
        ],
        compiler_params=pltpu.CompilerParams(vmem_limit_bytes=VMEM),
        cost_estimate=BACK_COST,
        name="back_first",
    )(own_question, own_blocks, enc_rank.reshape(1), order_row, *after, key_value, gathered, stats)


def back_second(own_question, own_blocks, key_value, gathered, norms, per_step=4):
    heads, tokens, pair_width = key_value.shape
    return pl.pallas_call(
        back_second_kernel,
        grid_spec=pltpu.PrefetchScalarGridSpec(
            num_scalar_prefetch=2,
            grid=(8 // per_step,),
            in_specs=back_specs(key_value, gathered, 1, per_step)
            + [pl.BlockSpec(norms.shape, lambda i, *_: (0, 0, 0))],
            out_specs=pl.BlockSpec((tokens, per_step * pair_width), lambda i, *_: (0, i)),
        ),
        out_shape=jax.ShapeDtypeStruct((tokens, 8 * pair_width), BF16),
        compiler_params=pltpu.CompilerParams(vmem_limit_bytes=VMEM),
        cost_estimate=BACK_COST,
        name="back_second",
    )(own_question, own_blocks, key_value, gathered, norms)


def product(near_ref, far_ref, own_ref, other_ref):
    rows, depth = SIDE * 128, near_ref.shape[-1]
    total = jnp.dot(near_ref[...].reshape(rows, depth), own_ref[...], preferred_element_type=F32)
    return total + jnp.dot(
        far_ref[...].reshape(rows, depth), other_ref[...], preferred_element_type=F32
    )


def chunk_spec(part, tokens, which):
    if part == 0:
        return pl.BlockSpec((1, SIDE, 128, tokens), lambda i, w: (w[which], 0, 0, 0))
    return pl.BlockSpec((SIDE, 1, 128, tokens), lambda i, w: (0, w[which], 0, 0))


def ordered(kernel, which_ref, after_ref, also_ref, *refs):
    kernel(which_ref, *refs)


def chunk_call(
    kernel, name, which, part, turned, grads, after, extra, extra_specs, out_specs, out_shape
):
    after = after if isinstance(after, tuple) else (after, after)
    tokens, columns = grads[0].shape
    half = pl.BlockSpec((tokens, columns // 2), lambda i, w: (0, i))
    chunks = which.shape[0]
    turned_specs, turned_args = [], []
    for index in range(chunks):
        turned_specs += [chunk_spec(part, tokens, index)] * 2
        turned_args += turned
    return pl.pallas_call(
        functools.partial(ordered, kernel),
        grid_spec=pltpu.PrefetchScalarGridSpec(
            num_scalar_prefetch=1,
            grid=(2,),
            in_specs=[pl.BlockSpec(memory_space=pl.ANY)] * 2
            + turned_specs
            + [half, half]
            + extra_specs,
            out_specs=out_specs,
        ),
        out_shape=out_shape,
        compiler_params=pltpu.CompilerParams(vmem_limit_bytes=VMEM),
        cost_estimate=small_cost(),
        name=name,
    )(which, *after, *turned_args, *grads, *extra)


def far_kernel(which_ref, near_ref, far_ref, own_ref, other_ref, a_ref, b_ref):
    total = product(near_ref, far_ref, own_ref, other_ref).astype(BF16)

    @pl.when(pl.program_id(0) == 0)
    def _():
        a_ref[...] = total

    @pl.when(pl.program_id(0) == 1)
    def _():
        b_ref[...] = total


def far_chunk(which, part, turned, grads, after):
    rows, columns = SIDE * 128, grads[0].shape[1] // 2
    half = jax.ShapeDtypeStruct((rows, columns), BF16)
    half_spec = pl.BlockSpec((rows, columns), lambda i, w: (0, 0))
    return chunk_call(
        far_kernel, "far_chunk", which, part, turned, grads, after, [], [], [half_spec] * 2, [half] * 2
    )


def own_kernel(which_ref, near_ref, far_ref, own_ref, other_ref, o_ref):
    o_ref[0] = product(near_ref, far_ref, own_ref, other_ref).astype(BF16)


def own_chunk(which, part, turned, grads, after):
    rows, columns = SIDE * 128, grads[0].shape[1] // 2
    return chunk_call(
        own_kernel,
        "own_chunk",
        which,
        part,
        turned,
        grads,
        after,
        [],
        [],
        pl.BlockSpec((1, rows, columns), lambda i, w: (i, 0, 0)),
        jax.ShapeDtypeStruct((2, rows, columns), BF16),
    )


def side_kernel(
    which_ref, up_near, up_far, down_near, down_far, own_ref, other_ref, a_ref, b_ref, up_ref, down_ref
):
    first = pl.program_id(0) == 0
    zero = jnp.zeros(a_ref.shape, F32)
    up = product(up_near, up_far, own_ref, other_ref)
    up_ref[0] = (up + jnp.where(first, a_ref[...].astype(F32), zero)).astype(BF16)
    down = product(down_near, down_far, own_ref, other_ref)
    down_ref[0] = (down + jnp.where(first, zero, b_ref[...].astype(F32))).astype(BF16)


def side_chunks(which, part, turned, grads, after, came):
    rows, columns = SIDE * 128, grads[0].shape[1] // 2
    both = jax.ShapeDtypeStruct((2, rows, columns), BF16)
    out = pl.BlockSpec((1, rows, columns), lambda i, w: (i, 0, 0))
    full = pl.BlockSpec((rows, columns), lambda i, w: (0, 0))
    return chunk_call(
        side_kernel, "side_chunks", which, part, turned, grads, after, list(came), [full, full], [out, out], [both, both]
    )


def total_kernel(which_ref, after_ref, also_ref, own_ref, up_ref, down_ref, *out_refs):
    total = own_ref[...].astype(F32) + up_ref[...].astype(F32) + down_ref[...].astype(F32)
    for step, ref in enumerate(out_refs):

        @pl.when(pl.program_id(0) == step)
        def _():
            ref[...] = total[:, 0].astype(BF16)


def totals(first, after, own, up, down):
    columns = own.shape[-1]
    cut = lambda a: a.reshape(2, SIDE, 128, columns)
    block = pl.BlockSpec((2, 1, 128, columns), lambda i, w: (0, (w[0] + i) % SIDE, 0, 0))
    out = pl.BlockSpec((2, 128, columns), lambda i, w: (0, 0, 0))
    return pl.pallas_call(
        total_kernel,
        grid_spec=pltpu.PrefetchScalarGridSpec(
            num_scalar_prefetch=1,
            grid=(SIDE,),
            in_specs=[pl.BlockSpec(memory_space=pl.ANY)] * 2 + [block] * 3,
            out_specs=[out] * SIDE,
        ),
        out_shape=[jax.ShapeDtypeStruct((2, 128, columns), BF16)] * SIDE,
        compiler_params=pltpu.CompilerParams(vmem_limit_bytes=VMEM),
        cost_estimate=small_cost(),
        name="totals",
    )(first.reshape(1), *after, cut(own), cut(up), cut(down))


def gather_terms(refs):
    return sum(r[...].astype(F32) for r in refs).astype(BF16)


def first_kernel(after_ref, *refs):
    refs[-1][...] = gather_terms(refs[:-1])


def first_half(after, pieces):
    block = pl.BlockSpec(pieces[0].shape, lambda: (0, 0, 0))
    return pl.pallas_call(
        first_kernel,
        in_specs=[pl.BlockSpec(memory_space=pl.ANY)] + [block] * len(pieces),
        out_specs=block,
        out_shape=jax.ShapeDtypeStruct(pieces[0].shape, BF16),
        compiler_params=pltpu.CompilerParams(vmem_limit_bytes=VMEM),
        cost_estimate=small_cost(),
        name="first_half",
    )(after, *pieces)


def finish_kernel(first_ref, *refs):
    heads = []
    for total in (first_ref[...], gather_terms(refs[:-1])):
        for half in range(2):
            for head in range(4):
                heads.append(total[half, :, head * 128 : (head + 1) * 128])
    refs[-1][...] = jnp.swapaxes(jnp.stack(heads), 0, 1)


def finish(first, pieces):
    return pl.pallas_call(
        finish_kernel,
        out_shape=jax.ShapeDtypeStruct((128, 16, 128), BF16),
        compiler_params=pltpu.CompilerParams(vmem_limit_bytes=VMEM),
        cost_estimate=small_cost(),
        name="finish",
    )(first, *pieces)


def by_token_kernel(after_ref, a_ref, b_ref, o_ref):
    heads = [ref[:, h * 128 : (h + 1) * 128] for ref in (a_ref, b_ref) for h in range(8)]
    o_ref[...] = jnp.swapaxes(jnp.stack(heads), 0, 1)


def by_token(after, a, b, rows=128):
    tokens, columns = a.shape
    block = pl.BlockSpec((rows, columns), lambda i: (i, 0))
    return pl.pallas_call(
        by_token_kernel,
        grid=(tokens // rows,),
        in_specs=[pl.BlockSpec(memory_space=pl.ANY), block, block],
        out_specs=pl.BlockSpec((rows, 16, 128), lambda i: (i, 0, 0)),
        out_shape=jax.ShapeDtypeStruct((tokens, 16, 128), BF16),
        compiler_params=pltpu.CompilerParams(vmem_limit_bytes=VMEM),
        cost_estimate=small_cost(),
        name="by_token",
    )(after, a, b)


def add_after(after, a, b):
    a, after = lax.optimization_barrier((a, after))
    return add(a, b)


def gap_kernel(heads_rows, rank_ref, aux_ref, m1_ref, m2_ref, m3_ref, part_ref, gate_ref, keep_ref, give_ref):
    rows = keep_ref.shape[0]
    mass = (aux_ref[0:2] + m1_ref[0:2]) + (m2_ref[0:2] + m3_ref[0:2])
    gap = aux_ref[2:4] - mass / heads_rows
    rank = rank_ref[0]

    def at(place):
        here = pl.ds(pl.multiple_of(place * rows, 8), rows)
        return gap[0:1, 0:1] * part_ref[0, here, :] + gap[1:2, 0:1] * part_ref[1, here, :]

    keep_ref[...] = at(rank)
    give_ref[...] = at(1 - rank).astype(BF16)


def apply_gap(ret_rank, aux, masses, parts, heads_rows, gate):
    _, rows, columns = parts.shape
    whole = lambda *shape: pl.BlockSpec(shape, lambda i, r: (0,) * len(shape))
    return pl.pallas_call(
        functools.partial(gap_kernel, float(heads_rows)),
        grid_spec=pltpu.PrefetchScalarGridSpec(
            num_scalar_prefetch=1,
            grid=(1,),
            in_specs=[whole(8, 128)] * 4
            + [whole(2, rows, columns), pl.BlockSpec(memory_space=pl.ANY)],
            out_specs=[whole(rows // 2, columns)] * 2,
        ),
        out_shape=[
            jax.ShapeDtypeStruct((rows // 2, columns), F32),
            jax.ShapeDtypeStruct((rows // 2, columns), BF16),
        ],
        compiler_params=pltpu.CompilerParams(vmem_limit_bytes=VMEM),
        cost_estimate=small_cost(),
        name="apply_gap",
    )(ret_rank.reshape(1), aux, *masses, parts, gate)


def ring_pairs(axis, step):
    pairs = []
    for x in range(SIDE):
        for y in range(SIDE):
            to = ((x + step) % SIDE, y) if axis == 0 else (x, (y + step) % SIDE)
            pairs.append((x * SIDE + y, to[0] * SIDE + to[1]))
    return pairs


def send(value, axis, step):
    return lax.ppermute(value, "enc", ring_pairs(axis, step))


def add(*terms):
    return sum(t.astype(F32) for t in terms).astype(BF16)


def join_kernel(low_ref, after_ref, own_ref, far_ref, o_ref):
    rows = own_ref.shape[0]
    low = low_ref[0] == 1
    own, far = own_ref[...], far_ref[...]
    o_ref[:rows] = jnp.where(low, own, far)
    o_ref[rows:] = jnp.where(low, far, own)


def joined(after, block, far, bit, rank):
    rows, columns = block.shape
    low = ((rank & bit) == 0).astype(jnp.int32).reshape(1)
    half = pl.BlockSpec((rows, columns), lambda i, r: (0, 0))
    return pl.pallas_call(
        join_kernel,
        grid_spec=pltpu.PrefetchScalarGridSpec(
            num_scalar_prefetch=1,
            grid=(1,),
            in_specs=[pl.BlockSpec(memory_space=pl.ANY), half, half],
            out_specs=pl.BlockSpec((2 * rows, columns), lambda i, r: (0, 0)),
        ),
        out_shape=jax.ShapeDtypeStruct((2 * rows, columns), block.dtype),
        compiler_params=pltpu.CompilerParams(vmem_limit_bytes=VMEM),
        cost_estimate=small_cost(),
        name="join",
    )(low, after, block, far)


def doubled(block, axis, bit, rank):
    size = lax.axis_size(axis)
    far = lax.ppermute(block, axis, [(i, i ^ bit) for i in range(size)])
    low = (rank & bit) == 0
    return jnp.concatenate([jnp.where(low, block, far), jnp.where(low, far, block)])


def on_device(
    enc_states,
    kv_weight,
    queries,
    out_grad,
    passage_order,
    passage_blocks,
    ret_tokens,
    ret_weight,
    question_emb,
):
    pass_dev, _, slot_len, width = enc_states.shape
    heads, pair_width = kv_weight.shape[1:]
    question_count, query_len = queries.shape[:2]
    enc_rank = lax.axis_index("enc")
    dec_rank = lax.axis_index("dec")
    ret_rank = lax.axis_index("ret")
    order_row = passage_order[0]
    blocks_row = passage_blocks[0]
    tokens = pass_dev * slot_len
    swap = [(0, 1), (1, 0)]

    rows = question_count * query_len
    packed = pack(order_row, queries.reshape(rows, HD), out_grad.reshape(rows, HD))
    gathered = lax.all_to_all(
        packed.reshape(N_ENC, pass_dev * query_len, pair_width),
        "enc",
        split_axis=0,
        concat_axis=0,
        tiled=True,
    )

    tok_rows = enc_states.reshape(tokens, width)
    key_value = project(tok_rows, kv_weight)

    own_pass = enc_rank * pass_dev + jnp.arange(pass_dev, dtype=jnp.int32)
    slot_of = jnp.sum(
        jnp.where(
            order_row[None, :] == own_pass[:, None],
            jnp.arange(order_row.shape[0], dtype=jnp.int32)[None, :],
            0,
        ),
        axis=1,
    )
    own_question = slot_of // PASS
    own_blocks = lax.dynamic_slice_in_dim(blocks_row, enc_rank * pass_dev, pass_dev)
    own_emb = jnp.sum(
        jnp.where(
            (own_question[:, None] == jnp.arange(question_count)[None, :])[..., None],
            question_emb[None],
            0.0,
        ),
        axis=1,
    )
    ret_rows = ret_tokens.reshape(tokens, ret_tokens.shape[3])
    ret_width = ret_rows.shape[1]
    pre_act = jnp.dot(ret_rows, ret_weight, preferred_element_type=F32).reshape(
        pass_dev, slot_len, ret_width
    )
    own_live = jnp.arange(slot_len, dtype=jnp.int32)[None, :] < BLK * own_blocks[:, None]
    own_length = (BLK * own_blocks).astype(F32)
    embed_own = (
        jnp.sum(jnp.where(own_live[..., None], jax.nn.gelu(pre_act), 0.0), axis=1)
        / own_length[:, None]
    )
    own_score = jnp.sum(own_emb * embed_own, axis=-1)
    score_rows = jnp.broadcast_to(
        jnp.concatenate([own_score, jnp.zeros((8 - pass_dev,), F32)])[:, None], (8, 128)
    )

    stats, late_emb = local_stats(
        own_question, own_blocks, key_value, gathered, score_rows, own_emb
    )
    mine, to_send = turn(ret_rank, stats, tok_rows)
    other = lax.ppermute(to_send, "ret", swap)
    hidden_grad = jnp.where(
        own_live[..., None], (late_emb / own_length[:, None])[:, None, :], 0.0
    )
    pre_grad = gelu_grad(pre_act, hidden_grad).astype(BF16)
    share = ret_width // N_DEC
    part_rows = lax.dynamic_slice_in_dim(ret_rows, dec_rank * share, share, axis=1)
    ret_parts = lax.dot_general(
        part_rows.reshape(pass_dev, slot_len, share),
        pre_grad,
        (((1,), (1,)), ((0,), (0,))),
        preferred_element_type=F32,
    )
    stats_all = lax.all_to_all(stats, "enc", split_axis=0, concat_axis=0, tiled=True)
    flat_a, norms, aux = back_first(
        (ret_parts, other), own_question, own_blocks, enc_rank, order_row, key_value, gathered, stats_all
    )
    far_a = lax.ppermute(flat_a, "ret", swap)
    flat_b = back_second(own_question, own_blocks, key_value, gathered, norms)
    far_b = lax.ppermute(flat_b, "ret", swap)

    turned = [
        mine.reshape(SIDE, SIDE, 128, tokens),
        other.reshape(SIDE, SIDE, 128, tokens),
    ]
    grads = [[flat_a, far_a], [flat_b, far_b]]
    at = (enc_rank // SIDE, enc_rank % SIDE)
    steps = lambda part, *ks: (at[part] + jnp.array(ks, jnp.int32)) % SIDE
    def level(after, half, bit):
        far = lax.ppermute(half, "enc", [(i, i ^ bit) for i in range(N_ENC)])
        return add_after(after, half, far)

    masses = [
        lax.ppermute(aux, "dec", [(i, (i + step) % N_DEC) for i in range(N_DEC)])
        for step in range(1, N_DEC)
    ]
    keep, give = apply_gap(
        ret_rank, aux, masses, ret_parts, N_DEC * heads * query_len, flat_b
    )
    half = add(keep, lax.ppermute(give, "ret", swap))
    a, b = far_chunk(steps(0, 2), 0, turned, grads[0], half)
    came = [(send(a, 0, 1), send(b, 0, -1))]
    half = level(a, half, 1)
    a, b = far_chunk(steps(1, 2), 1, turned, grads[1], half)
    came.append((send(a, 1, 1), send(b, 1, -1)))
    half = level(a, half, 4)
    up, down = side_chunks(steps(0, 1, 3), 0, turned, grads[0], half, came[0])
    sent = [(send(up, 0, 1), send(down, 0, -1))]
    half = level(up, half, 8)
    up, down = side_chunks(steps(1, 1, 3), 1, turned, grads[1], half, came[1])
    sent.append((send(up, 1, 1), send(down, 1, -1)))
    half = level(up, half, 2)
    own = [own_chunk(steps(0, 0), 0, turned, grads[0], up)]
    own.append(own_chunk(steps(1, 0), 1, turned, grads[1], own[0]))
    quarter = doubled(half, "ret", 1, ret_rank)
    far = lax.ppermute(quarter, "dec", [(i, i ^ 1) for i in range(N_DEC)])
    pieces, last = [], (own[1], own[1])
    for part in range(2):
        cuts = totals(at[1 - part], last, own[part], *sent[part])
        pieces.append([cuts[0]] + [send(cuts[k], 1 - part, k) for k in range(1, SIDE)])
        if part == 0:
            ret_half = joined(cuts[0], quarter, far, 1, dec_rank)
            by_tokens = by_token(cuts[0], flat_a, flat_b)
        last = (by_tokens, ret_half)
    ret_weight_grad = doubled(ret_half, "dec", 2, dec_rank)
    kv_grad = by_tokens.reshape(
        pass_dev, 1, slot_len, heads, pair_width
    )
    summed = first_half(ret_weight_grad, pieces[0])
    weight_total = finish(summed, pieces[1])

    return (kv_grad, weight_total, ret_weight_grad)


def solution(mesh):
    return jax.shard_map(
        on_device,
        mesh=mesh,
        in_specs=(
            P("enc", "ret", None, None),
            P(None, "dec", None),
            P("ret", None, ("dec", "enc"), None),
            P("ret", None, ("dec", "enc"), None),
            P("ret", None),
            P("ret", None),
            P("enc", "ret", None, None),
            P(),
            P("ret", None),
        ),
        out_specs=(P("enc", "ret", None, "dec", None), P(("enc", "ret"), "dec", None), P()),
        check_vma=False,
    )
```
